256 devices in a mesh: col: 32 (over y, z), dom: 8 (over x, core).
Axes of the slice: x: 4, y: 4, z: 8, core: 2. Of those that a mesh axis runs over, the one named last changes fastest.
Arguments:
- source_feats: bfloat16 [65536, 128], P(('col', 'dom')), may hold values from -6 to 6
- source_scale: float32 [65536], P(('col', 'dom')), may hold values from 0.3 to 1
- dest_scale: float32 [32768], P(('col', 'dom')), may hold values from 0.01 to 0.1
- weight: bfloat16 [128, 256], replicated, may hold values from -0.5 to 0.5
- layer_bias: float32 [256], replicated, may hold values from -3 to 3
- tile_rows: int32 [40960], P(('col', 'dom')), may hold values from 0 to 31
- tile_cols: int32 [40960], P(('col', 'dom')), may hold values from 0 to 15
- tile_mask: int32 [40960, 128, 128], P(('col', 'dom')), may hold values 0 or 1
- targets: int32 [8192], P(('col', 'dom')), may hold values from 0 to 127
- upstream: bfloat16 [8192, 256], P(('col', 'dom')), may hold values from -6 to 6
Outputs:
- hidden: bfloat16 [32768, 256], P(('col', 'dom'))
- weight_grad: float32 [128, 256], replicated
- bias_grad: float32 [256], replicated
- input_grad: float32 [65536, 128], P(('col', 'dom'))
The draws below stay inside these ranges and needn't reach their ends.
Inputs may be any that keep to these rules, and one draw needn't show every extreme that they name: `tile_rows`: block of the tile among the 32 blocks of its destination partition; some blocks are named far more often than others. `tile_cols`: block of the tile among the 16 blocks of its source group. `targets`: a row of the device's own 128 destination rows; a row may be named more than once.
All inputs are finite; a program needn't handle non-finite values. No bound on the sum of `tile_mask` on one device may be relied on, other than what follows from the above.
Results may differ from the reference program's by a relative error of at most 0.03.
Values may be sent and summed in bfloat16 or wider, within the bound.
No kernel may reach another device: no remote copies, remote signals or barrier semaphores. Data moves between devices by JAX's collectives and lax.ppermute only.
A program may use at most 128 MiB of HBM per device.

```python
import math
import jax
import jax.numpy as jnp
import numpy as np
from jax import lax

F = 128
HID = 256
BLK = 128
DST_DEV = 128
SRC_DEV = 256
TILES_DEV = 160
TGT_DEV = 32
NDST = 32768
NSRC = 65536
TILES = 40960
TGTS = 8192
N_COL = 32
N_DOM = 8


def set_ends(drawn, rng, low, largest):
    index_at = [jax.random.randint(jax.random.fold_in(rng, axis), (), 0, length) for axis, length in enumerate(drawn.shape)]
    main_axis = drawn.shape.index(max(drawn.shape))
    next_to = index_at[:main_axis] + [(index_at[main_axis] + 1) % drawn.shape[main_axis]] + index_at[main_axis + 1:]
    return drawn.at[tuple(index_at)].set(low).at[tuple(next_to)].set(largest)


def steps_of(rng, shape, pieces, smallest, top_value):
    level = 1.0
    for dim, blocks in pieces:
        steps = jax.random.uniform(jax.random.fold_in(jax.random.fold_in(rng, 6), dim), (blocks,), jnp.float32, smallest / len(pieces), top_value / len(pieces))
        level = level * jnp.repeat(jnp.exp(steps), shape[dim] // blocks).reshape((-1,) + (1,) * (len(shape) - 1 - dim))
    return level


def rank_bounds(number_of, slope):
    weights = [(1 << 20) // math.isqrt(grade ** slope) + 1 for grade in range(1, number_of + 1)]
    spread = 1 + sum(weights) // (1 << 30)
    return np.cumsum(np.array([max(1, weight // spread) for weight in weights]))


def skewed_ids(rng, shape, amount, slope):
    grid = rank_bounds(amount, slope)
    pick = jax.random.randint(jax.random.fold_in(rng, 1), shape, 0, int(grid[amount - 1]))
    grade = jnp.searchsorted(jnp.asarray(grid, jnp.int32), pick, side="right")
    return jax.random.permutation(jax.random.fold_in(rng, 2), amount)[grade].astype(jnp.int32)


def gaussian(key, shape, scale, bound, pieces=(), kind=jnp.bfloat16):
    level = steps_of(key, shape, pieces, -0.22, 0.18) if pieces else 1.0
    result = jax.random.normal(key, shape, jnp.float32) * scale * level
    return jnp.minimum(jnp.maximum(result, -bound), bound).astype(kind)


def setup_inputs(seed: int = 0) -> dict:
    key_list = jax.random.split(jax.random.key(seed), 11)
    source_feats = gaussian(key_list[0], (NSRC, F), 1.0, 6.0, ((0, 256),))
    source_scale = jnp.clip(jnp.exp(math.log(1.0) - 1.2039728 * jax.random.uniform(key_list[1], (NSRC,), jnp.float32) ** steps_of(key_list[1], (NSRC,), ((0, 256),), -0.2, 0.2)), 0.3, 1.0)
    dest_scale = jnp.clip(jnp.exp(math.log(0.1) - 2.3025851 * jax.random.uniform(key_list[2], (NDST,), jnp.float32) ** steps_of(key_list[2], (NDST,), ((0, 256),), -0.2, 0.2)), 0.01, 0.1)
    weight = gaussian(key_list[3], (F, HID), F ** -0.5, 0.5)
    layer_bias = gaussian(key_list[4], (HID,), 0.5, 3.0, (), jnp.float32)
    tile_rows = set_ends(skewed_ids(key_list[5], (TILES,), N_COL * DST_DEV // BLK, 2), jax.random.fold_in(key_list[5], 3), 0, (N_COL * DST_DEV // BLK) - 1).astype(jnp.int32)
    tile_cols = set_ends(jax.random.randint(key_list[6], (TILES,), 0, N_DOM * SRC_DEV // BLK), jax.random.fold_in(key_list[6], 1), 0, (N_DOM * SRC_DEV // BLK) - 1).astype(jnp.int32)
    tile_mask = set_ends((jax.random.randint(key_list[7], (TILES, BLK, BLK), 0, 16) < 1).astype(jnp.int32), jax.random.fold_in(key_list[7], 1), 0, 1)
    targets = set_ends(jax.random.randint(key_list[8], (TGTS,), 0, DST_DEV), jax.random.fold_in(key_list[8], 1), 0, DST_DEV - 1).astype(jnp.int32)
    upstream = gaussian(key_list[9], (TGTS, HID), 1.0, 6.0, ((0, 256),))
    return dict(source_feats=source_feats, source_scale=source_scale, dest_scale=dest_scale, weight=weight, layer_bias=layer_bias, tile_rows=tile_rows, tile_cols=tile_cols, tile_mask=tile_mask, targets=targets, upstream=upstream)


def silu_slope(values):
    sigma = jax.nn.sigmoid(values)
    return sigma * (1.0 + values * (1.0 - sigma))


def tile_forward(source_part, row_ids, col_ids, edge_masks, row_blocks):
    picked = source_part[col_ids].astype(jnp.float32)
    product = jnp.einsum('tij,tjf->tif', edge_masks.astype(jnp.float32), picked)
    row_hot = (row_ids[:, None] == jnp.arange(row_blocks, dtype=jnp.int32)[None, :]).astype(jnp.float32)
    summed = jnp.einsum('tr,tif->rif', row_hot, product, precision=lax.Precision.HIGHEST)
    return summed.reshape(row_blocks * BLK, F)


def tile_backward(returned_part, row_ids, col_ids, edge_masks, col_blocks):
    picked = returned_part[row_ids].astype(jnp.float32)
    product = jnp.einsum('tij,tif->tjf', edge_masks.astype(jnp.float32), picked)
    col_hot = (col_ids[:, None] == jnp.arange(col_blocks, dtype=jnp.int32)[None, :]).astype(jnp.float32)
    summed = jnp.einsum('tc,tjf->cjf', col_hot, product, precision=lax.Precision.HIGHEST)
    return summed.reshape(col_blocks * BLK, F)


def reference(source_feats, source_scale, dest_scale, weight, layer_bias, tile_rows, tile_cols, tile_mask, targets, upstream):
    row_blocks = N_COL * DST_DEV // BLK
    col_blocks = N_DOM * SRC_DEV // BLK
    scaled = (source_feats.astype(jnp.float32) * source_scale[:, None]).astype(jnp.bfloat16)
    source_parts = scaled.reshape(N_COL, col_blocks, BLK, F)
    row_ids = tile_rows.reshape(N_COL, N_DOM, TILES_DEV)
    col_ids = tile_cols.reshape(N_COL, N_DOM, TILES_DEV)
    edge_masks = tile_mask.reshape(N_COL, N_DOM, TILES_DEV, BLK, BLK)

    def forward_step(carry, items):
        source_part, rows_here, cols_here, masks_here = items
        partial_sums = jax.vmap(tile_forward, in_axes=(None, 0, 0, 0, None))(source_part, rows_here, cols_here, masks_here, row_blocks)
        rounded = lax.optimization_barrier(partial_sums.astype(jnp.bfloat16))
        return carry + rounded.astype(jnp.float32), None

    start_total = jnp.zeros((N_DOM, row_blocks * BLK, F), jnp.float32)
    total, _ = lax.scan(forward_step, start_total, (source_parts, row_ids, col_ids, edge_masks))
    summed = total.reshape(N_DOM, N_COL, DST_DEV, F).transpose(1, 0, 2, 3).reshape(NDST, F)
    aggregated = (summed * dest_scale[:, None]).astype(jnp.bfloat16)
    preact = jnp.dot(aggregated, weight, preferred_element_type=jnp.float32) + layer_bias[None, :]
    hidden = jax.nn.silu(preact).astype(jnp.bfloat16)

    global_rows = (jnp.arange(TGTS, dtype=jnp.int32) // TGT_DEV) * DST_DEV + targets.astype(jnp.int32)
    slope_grad = (upstream.astype(jnp.float32) * silu_slope(preact[global_rows])).astype(jnp.bfloat16)
    weight_grad = jnp.dot(aggregated[global_rows].T, slope_grad, preferred_element_type=jnp.float32)
    bias_grad = jnp.sum(slope_grad.astype(jnp.float32), axis=0)
    returned_term = jnp.dot(slope_grad, weight.T, preferred_element_type=jnp.float32)
    collected = jnp.zeros((NDST, F), jnp.float32).at[global_rows].add(returned_term)
    returned = (collected * dest_scale[:, None]).astype(jnp.bfloat16)
    returned_parts = returned.reshape(N_COL, N_DOM, DST_DEV, F).transpose(1, 0, 2, 3).reshape(N_DOM, row_blocks, BLK, F)

    def backward_step(items):
        rows_here, cols_here, masks_here = items
        terms = jax.vmap(tile_backward, in_axes=(0, 0, 0, 0, None))(returned_parts, rows_here, cols_here, masks_here, col_blocks)
        return jnp.sum(terms, axis=0)

    grad_sum = lax.map(backward_step, (row_ids, col_ids, edge_masks)).reshape(NSRC, F)
    input_grad = grad_sum * source_scale[:, None]
    return hidden, weight_grad, bias_grad, input_grad
```

```python
import jax
import jax.numpy as jnp
from jax import lax
from jax.experimental import pallas as pl
from jax.experimental.pallas import tpu as pltpu
from jax.sharding import PartitionSpec as P

NY, NZ, NX, NCORE = 4, 8, 4, 2
COL, DOM = NY * NZ, NX * NCORE
BLK = 128
F = 128
HID = 256
TGT = 32
VMEM = pl.BlockSpec(memory_space=pltpu.VMEM)
SMEM = pl.BlockSpec(memory_space=pltpu.SMEM)
PARAMS = pltpu.CompilerParams(vmem_limit_bytes=48 * 1024 * 1024)
F32, BF16 = jnp.float32, jnp.bfloat16
EXTRA = 32


def call(kernel, outs, ins, scratch=(), flops=0, moved=0):
    return pl.pallas_call(
        kernel,
        out_shape=outs,
        in_specs=ins,
        out_specs=[VMEM] * len(outs),
        scratch_shapes=list(scratch),
        compiler_params=PARAMS,
        cost_estimate=pl.CostEstimate(flops=flops, bytes_accessed=moved, transcendentals=0),
    )


def sds(shape, dtype):
    return jax.ShapeDtypeStruct(shape, dtype)


def exchange_dom(value, distance):
    pairs = [(i, i ^ distance) for i in range(DOM)]
    return lax.ppermute(value, "dom", pairs)


def exchange_y(value, distance):
    pairs = [(i, (((i // NZ) ^ distance) * NZ) + i % NZ) for i in range(COL)]
    return lax.ppermute(value, "col", pairs)


def forward_kernel(place, rows, cols, mask, *refs):
    pieces, outs = refs[:DOM], refs[DOM : DOM + NY]
    sources, totals = refs[DOM + NY :]
    my_y, my_dom = place[0], place[1]
    for k in range(DOM):
        at = my_dom ^ k
        sources[2 * at] = pieces[k][0:BLK, :]
        sources[2 * at + 1] = pieces[k][BLK:, :]
    totals[...] = jnp.zeros_like(totals)
    tiles = mask.shape[0]
    step = 4

    def tile_step(i, carry):
        products = []
        for u in range(step):
            t = i * step + u
            edges = mask[t].astype(F32).astype(BF16)
            products.append(
                jnp.dot(edges, sources[cols[t]], preferred_element_type=F32)
            )
        for u in range(step):
            r = rows[i * step + u]
            totals[r] = totals[r] + products[u]
        return carry

    lax.fori_loop(0, tiles // step, tile_step, 0)
    for k in range(NY):
        base = (my_y ^ k) * NZ
        for z in range(NZ):
            outs[k][z * BLK : (z + 1) * BLK, :] = totals[base + z].astype(BF16)


def y_sum_kernel(own, a, b, c, out):
    total = (own[...].astype(F32) + a[...].astype(F32)) + (b[...].astype(F32) + c[...].astype(F32))
    out[...] = total.astype(BF16)


def column(row):
    return jnp.transpose(jnp.broadcast_to(row, (BLK, BLK)))


def sigmoid(v):
    return 1.0 / (1.0 + jnp.exp(-v))


def dense_kernel(parts, dest_scale, weight, bias, targets, upstream, hidden, packed):
    summed = parts[0].astype(F32)
    for z in range(1, NZ):
        summed = summed + parts[z].astype(F32)
    scale = column(dest_scale[...])
    aggregated = (summed * scale).astype(BF16)
    w = weight[...]
    preact = jnp.dot(aggregated, w, preferred_element_type=F32) + bias[...]
    hidden[...] = (preact * sigmoid(preact)).astype(BF16)
    wanted = targets[...]
    row_ids = lax.broadcasted_iota(jnp.int32, (BLK, TGT), 0)
    chosen = (row_ids == wanted).astype(F32)
    chosen_b = chosen.astype(BF16)
    agg_t = lax.dot_general(
        chosen_b, aggregated, (((0,), (0,)), ((), ())), preferred_element_type=F32
    ).astype(BF16)
    pre_t = jnp.dot(agg_t, w, preferred_element_type=F32) + bias[...]
    s = sigmoid(pre_t)
    slope = (upstream[...].astype(F32) * (s * (1.0 + pre_t * (1.0 - s)))).astype(BF16)
    weight_part = lax.dot_general(
        agg_t, slope, (((0,), (0,)), ((), ())), preferred_element_type=F32
    )
    bias_part = jnp.sum(slope.astype(F32), axis=0, keepdims=True)
    term = lax.dot_general(
        slope, w, (((1,), (1,)), ((), ())), preferred_element_type=F32
    )
    same = lax.dot_general(
        chosen_b, chosen_b, (((0,), (0,)), ((), ())), preferred_element_type=F32
    )
    collected = jnp.dot(
        same, term, preferred_element_type=F32, precision=lax.Precision.HIGHEST
    )
    scale_t = lax.dot_general(
        chosen, scale, (((0,), (0,)), ((), ())), preferred_element_type=F32,
        precision=lax.Precision.HIGHEST,
    )
    k_row = lax.broadcasted_iota(jnp.int32, (TGT, TGT), 0)
    k_col = lax.broadcasted_iota(jnp.int32, (TGT, TGT), 1)
    earlier = jnp.sum(jnp.where(k_col < k_row, same, 0.0), axis=1, keepdims=True)
    returned = jnp.where(earlier > 0.0, 0.0, collected * scale_t).astype(BF16)
    names = jnp.concatenate([wanted.astype(F32), jnp.zeros((1, BLK - TGT), F32)], axis=1)
    bias_hi = bias_part.astype(BF16).astype(F32)
    bias_lo = bias_part - bias_hi
    sundry = jnp.concatenate(
        [
            names,
            bias_hi[:, :BLK],
            bias_hi[:, BLK:],
            bias_lo[:, :BLK],
            bias_lo[:, BLK:],
            jnp.zeros((3, BLK), F32),
        ],
        axis=0,
    )
    for c in range(COL):
        at, side = 8 * (c // 2), BLK * (c % 2)
        packed[c, 0:TGT, :] = returned
        chunk = weight_part[at : at + 8, side : side + BLK]
        packed[c, TGT : TGT + 16, :] = jnp.concatenate([chunk, sundry], axis=0).astype(BF16)


def split(value):
    high = value.astype(BF16)
    low = (value - high.astype(F32)).astype(BF16)
    return high, low


def joined(high, low):
    return high.astype(F32) + low.astype(F32)


def backward_kernel(place, rows, cols, mask, packed, own, other, returned, totals):
    my_core = place[2]
    row_ids = lax.broadcasted_iota(jnp.int32, (BLK, TGT), 0)

    def unpack(c, grads):
        extra = packed[c, TGT : TGT + 16, :].astype(F32)
        wanted = extra[8:9, :TGT].astype(jnp.int32)
        chosen = (row_ids == wanted).astype(BF16)
        returned[c] = lax.dot_general(
            packed[c, 0:TGT, :], chosen, (((0,), (1,)), ((), ())), preferred_element_type=F32
        ).astype(BF16)
        return grads + extra

    grads = lax.fori_loop(0, COL, unpack, jnp.zeros((16, BLK), F32))
    high, low = split(grads)
    for ref in (own, other):
        ref[NX * 256 : NX * 256 + 16, :] = high
        ref[NX * 256 + 16 :, :] = low
    totals[...] = jnp.zeros_like(totals)
    tiles = mask.shape[0]
    step = 4

    def tile_step(i, carry):
        products = []
        for u in range(step):
            t = i * step + u
            edges = mask[t].astype(F32).astype(BF16)
            products.append(
                jnp.dot(returned[rows[t]], edges, preferred_element_type=F32)
            )
        for u in range(step):
            c = cols[i * step + u]
            totals[c] = totals[c] + products[u]
        return carry

    lax.fori_loop(0, tiles // step, tile_step, 0)
    for x in range(NX):
        for half in range(2):
            rows_at = pl.ds(x * 256 + half * BLK, BLK)
            for ref, core in ((own, my_core), (other, 1 - my_core)):
                block = (x * NCORE + core) * 2 + half
                ref[rows_at, :] = jnp.transpose(totals[block]).astype(BF16)


def core_sum_kernel(place, own, got, *outs):
    my_x = place[3]
    at = NX * 256
    grads = joined(own[at : at + 16, :], own[at + 16 :, :]) + joined(
        got[at : at + 16, :], got[at + 16 :, :]
    )
    high, low = split(grads)
    for k in range(NX):
        rows_at = pl.ds(pl.multiple_of((my_x ^ k) * 256, 256), 256)
        total = own[rows_at, :].astype(F32) + got[rows_at, :].astype(F32)
        outs[k][0:256, :] = total.astype(BF16)
        outs[k][256:272, :] = high
        outs[k][272:, :] = low


def finish_kernel(a, b, c, d, source_scale, grad, chunks, bias):
    for half in range(2):
        at = slice(half * BLK, (half + 1) * BLK)
        total = (a[at, :].astype(F32) + b[at, :].astype(F32)) + (
            c[at, :].astype(F32) + d[at, :].astype(F32)
        )
        grad[at, :] = total * column(source_scale[:, at])
    parts = [joined(ref[256:272, :], ref[272:, :]) for ref in (a, b, c, d)]
    grads = (parts[0] + parts[1]) + (parts[2] + parts[3])
    for i in range(COL):
        chunks[i] = grads[0:8, :]
    bias[:, :BLK] = grads[9:10, :] + grads[11:12, :]
    bias[:, BLK:] = grads[10:11, :] + grads[12:13, :]


def body(
    source_feats,
    source_scale,
    dest_scale,
    weight,
    layer_bias,
    tile_rows,
    tile_cols,
    tile_mask,
    targets,
    upstream,
):
    my_col, my_dom = lax.axis_index("col"), lax.axis_index("dom")
    place = jnp.stack([my_col >> 3, my_dom, my_dom & 1, my_dom >> 1]).astype(jnp.int32)
    tiles = tile_mask.shape[0]
    scaled = (source_feats.astype(F32) * source_scale[:, None]).astype(BF16)
    pieces = [scaled] + [exchange_dom(scaled, k) for k in range(1, DOM)]
    partials = call(
        forward_kernel,
        [sds((NZ * BLK, F), BF16)] * NY,
        [SMEM] * 3 + [VMEM] * (1 + DOM),
        [pltpu.VMEM((DOM * 2, BLK, F), BF16), pltpu.VMEM((COL, BLK, F), F32)],
        flops=2 * tiles * BLK**3,
        moved=tiles * BLK * BLK * 4,
    )(place, tile_rows, tile_cols, tile_mask, *pieces)
    arrived = [exchange_y(partials[k], k) for k in range(1, NY)]
    (line,) = call(
        y_sum_kernel, [sds((NZ * BLK, F), BF16)], [VMEM] * NY, moved=5 * NZ * BLK * F * 2
    )(partials[0], *arrived)
    groups = [[y * NZ + z for z in range(NZ)] for y in range(NY)]
    parts = lax.all_to_all(
        line.reshape(NZ, BLK, F), "col", 0, 0, axis_index_groups=groups, tiled=True
    )
    hidden, packed = call(
        dense_kernel,
        [sds((BLK, HID), BF16), sds((COL, TGT + 16, F), BF16)],
        [VMEM] * 6,
    )(
        parts,
        dest_scale.reshape(1, BLK),
        weight,
        layer_bias.reshape(1, HID),
        targets.reshape(1, TGT),
        upstream,
    )
    gathered = lax.all_to_all(packed, "col", 0, 0, tiled=True)
    own, other = call(
        backward_kernel,
        [sds((NX * 256 + EXTRA, F), BF16)] * 2,
        [SMEM] * 3 + [VMEM] * 2,
        [pltpu.VMEM((COL, F, BLK), BF16), pltpu.VMEM((DOM * 2, F, BLK), F32)],
        flops=2 * tiles * BLK**3,
        moved=tiles * BLK * BLK * 4,
    )(place, tile_rows, tile_cols, tile_mask, gathered)
    got = exchange_dom(other, 1)
    by_x = call(
        core_sum_kernel, [sds((256 + EXTRA, F), BF16)] * NX, [SMEM, VMEM, VMEM]
    )(place, own, got)
    from_x = [exchange_dom(by_x[k], 2 * k) for k in range(1, NX)]
    input_grad, chunks, bias_grad = call(
        finish_kernel,
        [sds((256, F), F32), sds((COL, 8, BLK), F32), sds((1, HID), F32)],
        [VMEM] * 5,
    )(by_x[0], *from_x, source_scale.reshape(1, 256))
    spread = lax.all_to_all(chunks, "col", 0, 0, tiled=True)
    weight_grad = spread.reshape(F // 8, 2, 8, BLK).transpose(0, 2, 1, 3).reshape(F, HID)
    return hidden, weight_grad, bias_grad.reshape(HID), input_grad


def solution(mesh):
    placed = (
        P(("col", "dom"), None),
        P(("col", "dom")),
        P(("col", "dom")),
        P(),
        P(),
        P(("col", "dom")),
        P(("col", "dom")),
        P(("col", "dom"), None, None),
        P(("col", "dom")),
        P(("col", "dom"), None),
    )
    return jax.shard_map(
        body,
        mesh=mesh,
        in_specs=placed,
        out_specs=(P(("col", "dom"), None), P(), P(), P(("col", "dom"), None)),
        check_vma=False,
    )
```

```python
import jax
import jax.numpy as jnp
from jax import lax
from jax.experimental import pallas as pl
from jax.experimental.pallas import tpu as pltpu
from jax.sharding import PartitionSpec as P

NY, NZ, NX, NCORE = 4, 8, 4, 2
COL, DOM = NY * NZ, NX * NCORE
BLK = 128
F = 128
HID = 256
TGT = 32
VMEM = pl.BlockSpec(memory_space=pltpu.VMEM)
HBM = pl.BlockSpec(memory_space=pltpu.HBM)
SMEM = pl.BlockSpec(memory_space=pltpu.SMEM)
F32, BF16 = jnp.float32, jnp.bfloat16
PAIRS = 96
HALF_AT = 120
EMPTY = 160
STEP = 8
GRADS = HID + 16
PACK = TGT + 16
Y_GROUPS = [[y * NZ + z for y in range(NY)] for z in range(NZ)]
Z_GROUPS = [[y * NZ + z for z in range(NZ)] for y in range(NY)]
X_GROUPS = [[x * NCORE + core for x in range(NX)] for core in range(NCORE)]


def call(kernel, outs, ins, scratch=(), flops=0, moved=0, limit=16):
    return pl.pallas_call(
        kernel,
        out_shape=outs,
        in_specs=ins,
        out_specs=[VMEM] * len(outs),
        scratch_shapes=list(scratch),
        compiler_params=pltpu.CompilerParams(vmem_limit_bytes=limit * 1024 * 1024),
        cost_estimate=pl.CostEstimate(flops=flops, bytes_accessed=moved, transcendentals=0),
    )


def sds(shape, dtype):
    return jax.ShapeDtypeStruct(shape, dtype)


def exchange_dom(value, distance):
    pairs = [(i, i ^ distance) for i in range(DOM)]
    return lax.ppermute(value, "dom", pairs)


def swap(value, axis, groups=None):
    return lax.all_to_all(value, axis, 0, 0, axis_index_groups=groups, tiled=True)


def pair_of(pairs, edges, n):
    word = pairs[n]
    both = jnp.concatenate([edges[word & 255], edges[(word >> 8) & 255]], axis=1)
    return both, (word >> 16) & 15, (word >> 20) & 15, word >> 24


def forward_kernel(ids, mask, *refs):
    pieces, (out, kept, pairs) = refs[:DOM], refs[DOM : DOM + 3]
    sources, totals, staged, edges, waiting, mask_sems, kept_sems = refs[DOM + 3 :]
    steps = mask.shape[0] // STEP

    def mask_copy(i):
        at = pl.ds(i * STEP, STEP)
        return pltpu.make_async_copy(mask.at[at], staged.at[at], mask_sems.at[i])

    def kept_copy(i):
        at = pl.ds(i * STEP, STEP)
        return pltpu.make_async_copy(edges.at[at], kept.at[at], kept_sems.at[i])

    for i in range(steps):
        mask_copy(i).start()
    my_dom = lax.axis_index("dom")
    for k in range(DOM):
        at = my_dom ^ k
        sources[2 * at] = pieces[k][0:BLK, :]
        sources[2 * at + 1] = pieces[k][BLK:, :]
    totals[...] = jnp.zeros_like(totals)
    edges[EMPTY:, :, :] = jnp.zeros((STEP, BLK, BLK), BF16)
    kept_copy(steps).start()
    for r in range(COL):
        waiting[r] = -1

    def step(i, n):
        mask_copy(i).wait()
        products = []
        for u in range(STEP):
            t = i * STEP + u
            r, c = ids[t] >> 4, ids[t] & 15
            tile = staged[t].astype(F32).astype(BF16)
            edges[t] = tile
            products.append((r, jnp.dot(tile, sources[c], preferred_element_type=F32)))
            first = waiting[r]
            paired = first >= 0
            pairs[n] = (first & 255) | (t << 8) | ((first >> 8) << 16) | (c << 20) | (r << 24)
            waiting[r] = jnp.where(paired, -1, t | (c << 8))
            n = n + jnp.where(paired, 1, 0)
        for r, product in products:
            totals[r] = totals[r] + product
        kept_copy(i).start()
        return n

    n = lax.fori_loop(0, steps // 2, step, 0)
    pairs[HALF_AT] = n
    n = lax.fori_loop(steps // 2, steps, step, n)
    for r in range(COL):
        first = waiting[r]
        pairs[n] = (first & 255) | (EMPTY << 8) | ((first >> 8) << 16) | (r << 24)
        n = n + jnp.where(first >= 0, 1, 0)

    def fill(at, carry):
        pairs[at] = EMPTY | (EMPTY << 8)
        return carry

    lax.fori_loop(n, PAIRS, fill, 0)
    for r in range(COL):
        out[r] = totals[r].astype(BF16)
    for i in range(steps + 1):
        kept_copy(i).wait()


def forward(ids, tile_mask, pieces):
    tiles = tile_mask.shape[0]
    steps = tiles // STEP
    return pl.pallas_call(
        forward_kernel,
        out_shape=[
            sds((COL, BLK, F), BF16),
            sds((tiles + STEP, BLK, BLK), BF16),
            sds((BLK,), jnp.int32),
        ],
        in_specs=[SMEM, HBM] + [VMEM] * DOM,
        out_specs=[VMEM, HBM, SMEM],
        scratch_shapes=[
            pltpu.VMEM((DOM * 2, BLK, F), BF16),
            pltpu.VMEM((COL, BLK, F), F32),
            pltpu.VMEM(tile_mask.shape, jnp.int32),
            pltpu.VMEM((tiles + STEP, BLK, BLK), BF16),
            pltpu.SMEM((COL,), jnp.int32),
            pltpu.SemaphoreType.DMA((steps,)),
            pltpu.SemaphoreType.DMA((steps + 1,)),
        ],
        compiler_params=pltpu.CompilerParams(vmem_limit_bytes=52 * 1024 * 1024),
        cost_estimate=pl.CostEstimate(
            flops=2 * tiles * BLK**3, bytes_accessed=tiles * BLK * BLK * 6, transcendentals=0
        ),
    )(ids, tile_mask, *pieces)


def column(row):
    return jnp.transpose(jnp.broadcast_to(row, (BLK, BLK)))


def sigmoid(v):
    return 1.0 / (1.0 + jnp.exp(-v))


def y_sum_kernel(parts, out):
    for z in range(NZ):
        total = (parts[0, z].astype(F32) + parts[1, z].astype(F32)) + (
            parts[2, z].astype(F32) + parts[3, z].astype(F32)
        )
        out[z] = total.astype(BF16)


def dense_kernel(parts, dest_scale, weight, bias, targets, upstream, hidden, packed):
    summed = parts[0].astype(F32)
    for z in range(1, NZ):
        summed = summed + parts[z].astype(F32)
    scale = column(dest_scale[...])
    aggregated = (summed * scale).astype(BF16)
    w = weight[...]
    preact = jnp.dot(aggregated, w, preferred_element_type=F32) + bias[...]
    hidden[...] = (preact * sigmoid(preact)).astype(BF16)
    wanted = targets[...]
    row_ids = lax.broadcasted_iota(jnp.int32, (BLK, TGT), 0)
    chosen = (row_ids == wanted).astype(F32)
    chosen_b = chosen.astype(BF16)
    agg_t = lax.dot_general(
        chosen_b, aggregated, (((0,), (0,)), ((), ())), preferred_element_type=F32
    ).astype(BF16)
    pre_t = jnp.dot(agg_t, w, preferred_element_type=F32) + bias[...]
    s = sigmoid(pre_t)
    slope = (upstream[...].astype(F32) * (s * (1.0 + pre_t * (1.0 - s)))).astype(BF16)
    weight_part = lax.dot_general(
        agg_t, slope, (((0,), (0,)), ((), ())), preferred_element_type=F32
    )
    bias_part = jnp.sum(slope.astype(F32), axis=0, keepdims=True)
    term = lax.dot_general(
        slope, w, (((1,), (1,)), ((), ())), preferred_element_type=F32
    )
    same = lax.dot_general(
        chosen_b, chosen_b, (((0,), (0,)), ((), ())), preferred_element_type=F32
    )
    collected = jnp.dot(
        same, term, preferred_element_type=F32, precision=lax.Precision.HIGHEST
    )
    scale_t = lax.dot_general(
        chosen, scale, (((0,), (0,)), ((), ())), preferred_element_type=F32,
        precision=lax.Precision.HIGHEST,
    )
    k_row = lax.broadcasted_iota(jnp.int32, (TGT, TGT), 0)
    k_col = lax.broadcasted_iota(jnp.int32, (TGT, TGT), 1)
    earlier = jnp.sum(jnp.where(k_col < k_row, same, 0.0), axis=1, keepdims=True)
    returned = jnp.where(earlier > 0.0, 0.0, collected * scale_t).astype(BF16)
    names = jnp.concatenate([wanted.astype(F32)] * (BLK // TGT), axis=1)
    lanes = lax.broadcasted_iota(jnp.int32, (1, BLK), 1)
    names = jnp.where(lanes // TGT == (lax.axis_index("col") & 3), names, -1.0)
    high = bias_part.astype(BF16).astype(F32)
    low = bias_part - high
    sundry = jnp.concatenate(
        [names, high[:, :BLK], high[:, BLK:], low[:, :BLK], low[:, BLK:], jnp.zeros((3, BLK), F32)],
        axis=0,
    )
    for c in range(COL):
        at, side = 8 * (c // 2), BLK * (c % 2)
        chunk = weight_part[at : at + 8, side : side + BLK]
        packed[c, 0:TGT, :] = returned
        packed[c, TGT:, :] = jnp.concatenate([chunk, sundry], axis=0).astype(BF16)


def gradient_kernel(packed, chunks, bias):
    total = packed[0, TGT:, :].astype(F32)
    for c in range(1, COL):
        total = total + packed[c, TGT:, :].astype(F32)
    for c in range(COL):
        chunks[c] = total[0:8, :]
    bias[...] = jnp.concatenate([total[9:10] + total[11:12], total[10:11] + total[12:13]], axis=1)


def unpack(packed, returned):
    row_ids = lax.broadcasted_iota(jnp.int32, (BLK, BLK), 0).astype(F32)
    quarters = BLK // TGT
    for g in range(COL // quarters):
        held = slice(g * quarters, (g + 1) * quarters)
        rows = jnp.transpose(packed[held, 0:TGT, :].reshape(BLK, F))
        for first in range(g * quarters, (g + 1) * quarters, 2):
            chosen = [
                (row_ids == packed[c, TGT:, :].astype(F32)[8:9, :]).astype(BF16)
                for c in (first, first + 1)
            ]
            placed = lax.dot_general(
                rows,
                jnp.concatenate(chosen, axis=0),
                (((1,), (1,)), ((), ())),
                preferred_element_type=F32,
            ).astype(BF16)
            returned[first] = placed[:, :BLK]
            returned[first + 1] = placed[:, BLK:]


def bias_rows(bias):
    high = bias.astype(BF16).astype(F32)
    low = bias - high
    return jnp.concatenate(
        [high[:, :BLK], high[:, BLK:], low[:, :BLK], low[:, BLK:], jnp.zeros((12, BLK), F32)],
        axis=0,
    ).astype(BF16)


def bias_of(rows):
    rows = rows.astype(F32)
    return jnp.concatenate([rows[0:1] + rows[2:3], rows[1:2] + rows[3:4]], axis=1)


def backward_kernel(pairs, kept, packed, bias, own, other, edges, returned, totals, sems):
    my_core = lax.axis_index("dom") & 1
    copies = []
    for i in range(kept.shape[0] // STEP):
        at = pl.ds(i * STEP, STEP)
        copies.append(pltpu.make_async_copy(kept.at[at], edges.at[at], sems.at[i]))
        copies[-1].start()
    for ref in (own, other):
        ref[NX * 256 :, :] = bias_rows(bias[...])
    unpack(packed, returned)
    totals[...] = jnp.zeros_like(totals)
    half = len(copies) // 2
    for copy in copies[:half]:
        copy.wait()
    unroll = 4

    def pair_step(i, carry):
        products = []
        for u in range(unroll):
            both, c1, c2, r = pair_of(pairs, edges, i * unroll + u)
            products.append((c1, c2, jnp.dot(returned[r], both, preferred_element_type=F32)))
        for c1, c2, product in products:
            totals[c1] = totals[c1] + product[:, :BLK]
            totals[c2] = totals[c2] + product[:, BLK:]
        return carry

    early = pairs[HALF_AT] // unroll
    lax.fori_loop(0, early, pair_step, 0)
    for copy in copies[half:]:
        copy.wait()
    lax.fori_loop(early, PAIRS // unroll, pair_step, 0)
    for x in range(NX):
        for half in range(2):
            rows_at = pl.ds(x * 256 + half * BLK, BLK)
            for ref, core in ((own, my_core), (other, 1 - my_core)):
                block = (x * NCORE + core) * 2 + half
                ref[rows_at, :] = jnp.transpose(totals[block]).astype(BF16)


def core_sum_kernel(own, got, grads, grads_got, out):
    at = NX * 256
    bias = bias_rows(bias_of(own[at:, :]) + bias_of(got[at:, :]))
    weight_sum = [(grads[c] + grads_got[c]).astype(BF16) for c in range(COL)]
    for x in range(NX):
        rows_at = slice(x * 256, (x + 1) * 256)
        total = own[rows_at, :].astype(F32) + got[rows_at, :].astype(F32)
        out[x, 0:256, :] = total.astype(BF16)
        for c in range(0, COL, 2):
            out[x, 256 + 8 * c : 272 + 8 * c, :] = jnp.concatenate(weight_sum[c : c + 2], axis=0)
        out[x, 256 + HID :, :] = bias


def finish_kernel(parts, source_scale, grad, weight_grad, bias_grad):
    def total(at):
        return (parts[0, at, :].astype(F32) + parts[1, at, :].astype(F32)) + (
            parts[2, at, :].astype(F32) + parts[3, at, :].astype(F32)
        )

    for half in range(2):
        at = slice(half * BLK, (half + 1) * BLK)
        grad[at, :] = total(at) * column(source_scale[:, at])
    for c in range(0, COL, 2):
        both = total(slice(256 + 8 * c, 272 + 8 * c))
        rows_at = slice(4 * c, 4 * c + 8)
        weight_grad[rows_at, :BLK] = both[0:8]
        weight_grad[rows_at, BLK:] = both[8:16]
    bias = [bias_of(parts[x, 256 + HID :, :]) for x in range(NX)]
    bias_grad[...] = (bias[0] + bias[1]) + (bias[2] + bias[3])


def body(
    source_feats,
    source_scale,
    dest_scale,
    weight,
    layer_bias,
    tile_rows,
    tile_cols,
    tile_mask,
    targets,
    upstream,
):
    scaled = (source_feats.astype(F32) * source_scale[:, None]).astype(BF16)
    pieces = [scaled] + [exchange_dom(scaled, k) for k in range(1, DOM)]
    products = 2 * tile_mask.shape[0] * BLK**3
    partials, kept, pairs = forward(tile_rows * 16 + tile_cols, tile_mask, pieces)
    parts = swap(partials.reshape(NY, NZ, BLK, F), "col", Y_GROUPS)
    (line,) = call(y_sum_kernel, [sds((NZ, BLK, F), BF16)], [VMEM])(parts)
    parts = swap(line, "col", Z_GROUPS)
    hidden, packed = call(
        dense_kernel,
        [sds((BLK, HID), BF16), sds((COL, PACK, F), BF16)],
        [VMEM] * 6,
    )(
        parts,
        dest_scale.reshape(1, BLK),
        weight,
        layer_bias.reshape(1, HID),
        targets.reshape(1, TGT),
        upstream,
    )
    gathered = swap(packed, "col")
    chunks, bias_sum = call(
        gradient_kernel, [sds((COL, 8, BLK), F32), sds((1, HID), F32)], [VMEM]
    )(gathered)
    grads = swap(chunks, "col")
    own, other = call(
        backward_kernel,
        [sds((NX * 256 + 16, F), BF16)] * 2,
        [SMEM, HBM, VMEM, VMEM],
        [
            pltpu.VMEM(kept.shape, BF16),
            pltpu.VMEM((COL, F, BLK), BF16),
            pltpu.VMEM((DOM * 2, F, BLK), F32),
            pltpu.SemaphoreType.DMA((kept.shape[0] // STEP,)),
        ],
        flops=products,
        limit=52,
    )(pairs, kept, gathered, bias_sum)
    got = exchange_dom(other, 1)
    grads_got = exchange_dom(grads, 1)
    (by_x,) = call(core_sum_kernel, [sds((NX, 256 + GRADS, F), BF16)], [VMEM] * 4)(
        own, got, grads, grads_got
    )
    input_grad, weight_grad, bias_grad = call(
        finish_kernel,
        [sds((256, F), F32), sds((F, HID), F32), sds((1, HID), F32)],
        [VMEM] * 2,
    )(swap(by_x, "dom", X_GROUPS), source_scale.reshape(1, 256))
    return hidden, weight_grad, bias_grad.reshape(HID), input_grad


def solution(mesh):
    placed = (
        P(("col", "dom"), None),
        P(("col", "dom")),
        P(("col", "dom")),
        P(),
        P(),
        P(("col", "dom")),
        P(("col", "dom")),
        P(("col", "dom"), None, None),
        P(("col", "dom")),
        P(("col", "dom"), None),
    )
    return jax.shard_map(
        body,
        mesh=mesh,
        in_specs=placed,
        out_specs=(P(("col", "dom"), None), P(), P(), P(("col", "dom"), None)),
        check_vma=False,
    )
```

```python
import jax
import jax.numpy as jnp
from jax import lax
from jax.experimental import pallas as pl
from jax.experimental.pallas import tpu as pltpu
from jax.sharding import PartitionSpec as P

NY, NZ, NX, NCORE = 4, 8, 4, 2
COL, DOM = NY * NZ, NX * NCORE
BLK = 128
F = 128
HID = 256
TGT = 32
VMEM = pl.BlockSpec(memory_space=pltpu.VMEM)
HBM = pl.BlockSpec(memory_space=pltpu.HBM)
SMEM = pl.BlockSpec(memory_space=pltpu.SMEM)
F32, BF16 = jnp.float32, jnp.bfloat16
PAIRS = 96
UNROLL = 4
PHASES = 4
COUNT_AT = 112
EMPTY = 160
STEP = 8
GRADS = HID + 16
PACK = TGT + 16
Z_GROUPS = [[y * NZ + z for z in range(NZ)] for y in range(NY)]
X_GROUPS = [[x * NCORE + core for x in range(NX)] for core in range(NCORE)]


def call(kernel, outs, ins, scratch=(), flops=0, moved=0, limit=16):
    return pl.pallas_call(
        kernel,
        out_shape=outs,
        in_specs=ins,
        out_specs=[VMEM] * len(outs),
        scratch_shapes=list(scratch),
        compiler_params=pltpu.CompilerParams(vmem_limit_bytes=limit * 1024 * 1024),
        cost_estimate=pl.CostEstimate(flops=flops, bytes_accessed=moved, transcendentals=0),
    )


def sds(shape, dtype):
    return jax.ShapeDtypeStruct(shape, dtype)


def exchange_dom(value, distance):
    pairs = [(i, i ^ distance) for i in range(DOM)]
    return lax.ppermute(value, "dom", pairs)


def swap(value, axis, groups=None):
    return lax.all_to_all(value, axis, 0, 0, axis_index_groups=groups, tiled=True)


def pair_of(pairs, edges, n):
    word = pairs[n]
    both = jnp.concatenate([edges[word & 255], edges[(word >> 8) & 255]], axis=1)
    return both, (word >> 16) & 15, (word >> 20) & 15, word >> 24


def forward_kernel(ids, mask, *refs):
    pieces, (kept, pairs), outs = refs[:DOM], refs[DOM : DOM + 2], refs[DOM + 2 : DOM + 9]
    sources, totals, staged, edges, waiting, mask_sems, kept_sems = refs[DOM + 9 :]
    steps = mask.shape[0] // STEP

    def mask_copy(i):
        at = pl.ds(i * STEP, STEP)
        return pltpu.make_async_copy(mask.at[at], staged.at[at], mask_sems.at[i])

    def kept_copy(i):
        at = pl.ds(i * STEP, STEP)
        return pltpu.make_async_copy(edges.at[at], kept.at[at], kept_sems.at[i])

    for i in range(steps):
        mask_copy(i).start()
    my_dom = lax.axis_index("dom")
    for k in range(DOM):
        at = my_dom ^ k
        sources[2 * at] = pieces[k][0:BLK, :]
        sources[2 * at + 1] = pieces[k][BLK:, :]
    totals[...] = jnp.zeros_like(totals)
    edges[EMPTY:, :, :] = jnp.zeros((STEP, BLK, BLK), BF16)
    kept_copy(steps).start()
    for r in range(COL):
        waiting[r] = -1

    def step(i, n):
        mask_copy(i).wait()
        for u in range(STEP):
            t = i * STEP + u
            r, c = ids[t] >> 4, ids[t] & 15
            tile = staged[t].astype(F32).astype(BF16)
            edges[t] = tile
            totals[r] = totals[r] + jnp.dot(tile, sources[c], preferred_element_type=F32)
            first = waiting[r]
            paired = first >= 0
            pairs[n] = (first & 255) | (t << 8) | ((first >> 8) << 16) | (c << 20) | (r << 24)
            waiting[r] = jnp.where(paired, -1, t | (c << 8))
            n = n + jnp.where(paired, 1, 0)
        kept_copy(i).start()
        return n

    n = 0
    for phase in range(PHASES):
        n = lax.fori_loop(phase * steps // PHASES, (phase + 1) * steps // PHASES, step, n)
        pairs[COUNT_AT + phase] = n // UNROLL
    for r in range(COL):
        first = waiting[r]
        pairs[n] = (first & 255) | (EMPTY << 8) | ((first >> 8) << 16) | (r << 24)
        n = n + jnp.where(first >= 0, 1, 0)

    def fill(at, carry):
        pairs[at] = EMPTY | (EMPTY << 8)
        return carry

    lax.fori_loop(n, PAIRS, fill, 0)
    pairs[COUNT_AT + PHASES] = (n + UNROLL - 1) // UNROLL
    y = lax.axis_index("col") >> 3
    half = NZ // 2
    own, far_up, far_down, up_low, up_high, down_low, down_high = outs
    for out, step_to, first, count in (
        (far_up, 2, 0, half),
        (far_down, 2, half, half),
        (up_high, 1, half, half),
        (down_low, 3, 0, half),
        (up_low, 1, 0, half),
        (down_high, 3, half, half),
        (own, 0, 0, NZ),
    ):
        for z in range(count):
            out[z] = totals[((y + step_to) & 3) * NZ + first + z].astype(BF16)
    for i in range(steps + 1):
        kept_copy(i).wait()


def forward(ids, tile_mask, pieces):
    tiles = tile_mask.shape[0]
    steps = tiles // STEP
    return pl.pallas_call(
        forward_kernel,
        out_shape=[sds((tiles + STEP, BLK, BLK), BF16), sds((BLK,), jnp.int32)]
        + [sds((NZ, BLK, F), BF16)]
        + [sds((NZ // 2, BLK, F), BF16)] * 6,
        in_specs=[SMEM, HBM] + [VMEM] * DOM,
        out_specs=[HBM, SMEM] + [VMEM] * 7,
        scratch_shapes=[
            pltpu.VMEM((DOM * 2, BLK, F), BF16),
            pltpu.VMEM((COL, BLK, F), F32),
            pltpu.VMEM(tile_mask.shape, jnp.int32),
            pltpu.VMEM((tiles + STEP, BLK, BLK), BF16),
            pltpu.SMEM((COL,), jnp.int32),
            pltpu.SemaphoreType.DMA((steps,)),
            pltpu.SemaphoreType.DMA((steps + 1,)),
        ],
        compiler_params=pltpu.CompilerParams(vmem_limit_bytes=52 * 1024 * 1024),
        cost_estimate=pl.CostEstimate(
            flops=2 * tiles * BLK**3, bytes_accessed=tiles * BLK * BLK * 6, transcendentals=0
        ),
    )(ids, tile_mask, *pieces)


def column(row):
    return jnp.transpose(jnp.broadcast_to(row, (BLK, BLK)))


def sigmoid(v):
    return 1.0 / (1.0 + jnp.exp(-v))


def relay_kernel(up, far_up, down, far_down, out_up, out_down):
    for z in range(NZ // 2):
        out_up[z] = (up[z].astype(F32) + far_up[z].astype(F32)).astype(BF16)
        out_down[z] = (down[z].astype(F32) + far_down[z].astype(F32)).astype(BF16)


def y_sum_kernel(own, low_above, low_below, high_below, high_above, out):
    half = NZ // 2
    for z in range(half):
        low = low_above[z].astype(F32) + low_below[z].astype(F32)
        out[z] = (own[z].astype(F32) + low).astype(BF16)
        high = high_below[z].astype(F32) + high_above[z].astype(F32)
        out[z + half] = (own[z + half].astype(F32) + high).astype(BF16)


def step_y(value, step):
    pairs = [(i, ((i // NZ + step) % NY) * NZ + i % NZ) for i in range(COL)]
    return lax.ppermute(value, "col", pairs)


def dense_kernel(parts, dest_scale, weight, bias, targets, upstream, hidden, packed):
    summed = parts[0].astype(F32)
    for z in range(1, NZ):
        summed = summed + parts[z].astype(F32)
    scale = column(dest_scale[...])
    aggregated = (summed * scale).astype(BF16)
    w = weight[...]
    preact = jnp.dot(aggregated, w, preferred_element_type=F32) + bias[...]
    hidden[...] = (preact * sigmoid(preact)).astype(BF16)
    wanted = targets[...]
    row_ids = lax.broadcasted_iota(jnp.int32, (BLK, TGT), 0)
    chosen = (row_ids == wanted).astype(F32)
    chosen_b = chosen.astype(BF16)
    agg_t = lax.dot_general(
        chosen_b, aggregated, (((0,), (0,)), ((), ())), preferred_element_type=F32
    ).astype(BF16)
    pre_t = jnp.dot(agg_t, w, preferred_element_type=F32) + bias[...]
    s = sigmoid(pre_t)
    slope = (upstream[...].astype(F32) * (s * (1.0 + pre_t * (1.0 - s)))).astype(BF16)
    weight_part = lax.dot_general(
        agg_t, slope, (((0,), (0,)), ((), ())), preferred_element_type=F32
    )
    bias_part = jnp.sum(slope.astype(F32), axis=0, keepdims=True)
    term = lax.dot_general(
        slope, w, (((1,), (1,)), ((), ())), preferred_element_type=F32
    )
    same = lax.dot_general(
        chosen_b, chosen_b, (((0,), (0,)), ((), ())), preferred_element_type=F32
    )
    collected = jnp.dot(
        same, term, preferred_element_type=F32, precision=lax.Precision.HIGHEST
    )
    scale_t = lax.dot_general(
        chosen, scale, (((0,), (0,)), ((), ())), preferred_element_type=F32,
        precision=lax.Precision.HIGHEST,
    )
    k_row = lax.broadcasted_iota(jnp.int32, (TGT, TGT), 0)
    k_col = lax.broadcasted_iota(jnp.int32, (TGT, TGT), 1)
    earlier = jnp.sum(jnp.where(k_col < k_row, same, 0.0), axis=1, keepdims=True)
    returned = jnp.where(earlier > 0.0, 0.0, collected * scale_t).astype(BF16)
    names = jnp.concatenate([wanted.astype(F32)] * (BLK // TGT), axis=1)
    lanes = lax.broadcasted_iota(jnp.int32, (1, BLK), 1)
    names = jnp.where(lanes // TGT == (lax.axis_index("col") & 3), names, -1.0)
    high = bias_part.astype(BF16).astype(F32)
    low = bias_part - high
    sundry = jnp.concatenate(
        [names, high[:, :BLK], high[:, BLK:], low[:, :BLK], low[:, BLK:], jnp.zeros((3, BLK), F32)],
        axis=0,
    )
    for c in range(COL):
        at, side = 8 * (c // 2), BLK * (c % 2)
        chunk = weight_part[at : at + 8, side : side + BLK]
        packed[c, 0:TGT, :] = returned
        packed[c, TGT:, :] = jnp.concatenate([chunk, sundry], axis=0).astype(BF16)


def gradient_kernel(packed, chunks, bias):
    total = packed[0, TGT:, :].astype(F32)
    for c in range(1, COL):
        total = total + packed[c, TGT:, :].astype(F32)
    for c in range(COL):
        chunks[c] = total[0:8, :]
    bias[...] = jnp.concatenate([total[9:10] + total[11:12], total[10:11] + total[12:13]], axis=1)


def unpack(packed, returned):
    row_ids = lax.broadcasted_iota(jnp.int32, (BLK, BLK), 0).astype(F32)
    quarters = BLK // TGT
    for g in range(COL // quarters):
        held = slice(g * quarters, (g + 1) * quarters)
        rows = jnp.transpose(packed[held, 0:TGT, :].reshape(BLK, F))
        for first in range(g * quarters, (g + 1) * quarters, 2):
            chosen = [
                (row_ids == packed[c, TGT:, :].astype(F32)[8:9, :]).astype(BF16)
                for c in (first, first + 1)
            ]
            placed = lax.dot_general(
                rows,
                jnp.concatenate(chosen, axis=0),
                (((1,), (1,)), ((), ())),
                preferred_element_type=F32,
            ).astype(BF16)
            returned[first] = placed[:, :BLK]
            returned[first + 1] = placed[:, BLK:]


def bias_rows(bias):
    high = bias.astype(BF16).astype(F32)
    low = bias - high
    return jnp.concatenate(
        [high[:, :BLK], high[:, BLK:], low[:, :BLK], low[:, BLK:], jnp.zeros((12, BLK), F32)],
        axis=0,
    ).astype(BF16)


def bias_of(rows):
    rows = rows.astype(F32)
    return jnp.concatenate([rows[0:1] + rows[2:3], rows[1:2] + rows[3:4]], axis=1)


def backward_kernel(pairs, kept, packed, bias, own, other, edges, returned, totals, sems):
    my_core = lax.axis_index("dom") & 1
    last = kept.shape[0] // STEP - 1

    def kept_copy(i):
        at = pl.ds(i * STEP, STEP)
        return pltpu.make_async_copy(kept.at[at], edges.at[at], sems.at[i])

    for i in range(last + 1):
        kept_copy(i).start()
    for ref in (own, other):
        ref[NX * 256 :, :] = bias_rows(bias[...])
    unpack(packed, returned)
    totals[...] = jnp.zeros_like(totals)

    def step(g, carry):
        for u in range(UNROLL):
            both, c1, c2, r = pair_of(pairs, edges, g * UNROLL + u)
            product = jnp.dot(returned[r], both, preferred_element_type=F32)
            totals[c1] = totals[c1] + product[:, :BLK]
            totals[c2] = totals[c2] + product[:, BLK:]
        return carry

    done = 0
    for phase in range(PHASES):
        for i in range(phase * last // PHASES, (phase + 1) * last // PHASES):
            kept_copy(i).wait()
        until = pairs[COUNT_AT + phase]
        lax.fori_loop(done, until, step, 0)
        done = until
    kept_copy(last).wait()
    lax.fori_loop(done, pairs[COUNT_AT + PHASES], step, 0)
    for x in range(NX):
        for half in range(2):
            rows_at = pl.ds(x * 256 + half * BLK, BLK)
            for ref, core in ((own, my_core), (other, 1 - my_core)):
                block = (x * NCORE + core) * 2 + half
                ref[rows_at, :] = jnp.transpose(totals[block]).astype(BF16)


def core_sum_kernel(own, got, grads, grads_got, out):
    at = NX * 256
    bias = bias_rows(bias_of(own[at:, :]) + bias_of(got[at:, :]))
    weight_sum = [(grads[c] + grads_got[c]).astype(BF16) for c in range(COL)]
    for x in range(NX):
        rows_at = slice(x * 256, (x + 1) * 256)
        total = own[rows_at, :].astype(F32) + got[rows_at, :].astype(F32)
        out[x, 0:256, :] = total.astype(BF16)
        for c in range(0, COL, 2):
            out[x, 256 + 8 * c : 272 + 8 * c, :] = jnp.concatenate(weight_sum[c : c + 2], axis=0)
        out[x, 256 + HID :, :] = bias


def finish_kernel(parts, source_scale, grad, weight_grad, bias_grad):
    def total(at):
        return (parts[0, at, :].astype(F32) + parts[1, at, :].astype(F32)) + (
            parts[2, at, :].astype(F32) + parts[3, at, :].astype(F32)
        )

    for half in range(2):
        at = slice(half * BLK, (half + 1) * BLK)
        grad[at, :] = total(at) * column(source_scale[:, at])
    for c in range(0, COL, 2):
        both = total(slice(256 + 8 * c, 272 + 8 * c))
        rows_at = slice(4 * c, 4 * c + 8)
        weight_grad[rows_at, :BLK] = both[0:8]
        weight_grad[rows_at, BLK:] = both[8:16]
    bias = [bias_of(parts[x, 256 + HID :, :]) for x in range(NX)]
    bias_grad[...] = (bias[0] + bias[1]) + (bias[2] + bias[3])


def body(
    source_feats,
    source_scale,
    dest_scale,
    weight,
    layer_bias,
    tile_rows,
    tile_cols,
    tile_mask,
    targets,
    upstream,
):
    scaled = (source_feats.astype(F32) * source_scale[:, None]).astype(BF16)
    along_x = [scaled] + [exchange_dom(scaled, NCORE * k) for k in range(1, NX)]
    pieces = [piece for held in along_x for piece in (held, exchange_dom(held, 1))]
    products = 2 * tile_mask.shape[0] * BLK**3
    kept, pairs, own, far_up, far_down, up_low, up_high, down_low, down_high = forward(
        tile_rows * 16 + tile_cols, tile_mask, pieces
    )
    far_up, far_down = step_y(far_up, 1), step_y(far_down, -1)
    high_below, low_above = step_y(up_high, 1), step_y(down_low, -1)
    up, down = call(relay_kernel, [sds((NZ // 2, BLK, F), BF16)] * 2, [VMEM] * 4)(
        up_low, far_up, down_high, far_down
    )
    low_below, high_above = step_y(up, 1), step_y(down, -1)
    (line,) = call(y_sum_kernel, [sds((NZ, BLK, F), BF16)], [VMEM] * 5)(
        own, low_above, low_below, high_below, high_above
    )
    parts = swap(line, "col", Z_GROUPS)
    hidden, packed = call(
        dense_kernel,
        [sds((BLK, HID), BF16), sds((COL, PACK, F), BF16)],
        [VMEM] * 6,
    )(
        parts,
        dest_scale.reshape(1, BLK),
        weight,
        layer_bias.reshape(1, HID),
        targets.reshape(1, TGT),
        upstream,
    )
    gathered = swap(packed, "col")
    chunks, bias_sum = call(
        gradient_kernel, [sds((COL, 8, BLK), F32), sds((1, HID), F32)], [VMEM]
    )(gathered)
    grads = swap(chunks, "col")
    own, other = call(
        backward_kernel,
        [sds((NX * 256 + 16, F), BF16)] * 2,
        [SMEM, HBM, VMEM, VMEM],
        [
            pltpu.VMEM(kept.shape, BF16),
            pltpu.VMEM((COL, F, BLK), BF16),
            pltpu.VMEM((DOM * 2, F, BLK), F32),
            pltpu.SemaphoreType.DMA((kept.shape[0] // STEP,)),
        ],
        flops=products,
        limit=52,
    )(pairs, kept, gathered, bias_sum)
    got = exchange_dom(other, 1)
    grads_got = exchange_dom(grads, 1)
    (by_x,) = call(core_sum_kernel, [sds((NX, 256 + GRADS, F), BF16)], [VMEM] * 4)(
        own, got, grads, grads_got
    )
    input_grad, weight_grad, bias_grad = call(
        finish_kernel,
        [sds((256, F), F32), sds((F, HID), F32), sds((1, HID), F32)],
        [VMEM] * 2,
    )(swap(by_x, "dom", X_GROUPS), source_scale.reshape(1, 256))
    return hidden, weight_grad, bias_grad.reshape(HID), input_grad


def solution(mesh):
    placed = (
        P(("col", "dom"), None),
        P(("col", "dom")),
        P(("col", "dom")),
        P(),
        P(),
        P(("col", "dom")),
        P(("col", "dom")),
        P(("col", "dom"), None, None),
        P(("col", "dom")),
        P(("col", "dom"), None),
    )
    return jax.shard_map(
        body,
        mesh=mesh,
        in_specs=placed,
        out_specs=(P(("col", "dom"), None), P(), P(), P(("col", "dom"), None)),
        check_vma=False,
    )
```

```python
import jax
import jax.numpy as jnp
from jax import lax
from jax.experimental import pallas as pl
from jax.experimental.pallas import tpu as pltpu
from jax.sharding import PartitionSpec as P

NY, NZ, NX, NCORE = 4, 8, 4, 2
COL, DOM = NY * NZ, NX * NCORE
BLK = 128
F = 128
HID = 256
TGT = 32
VMEM = pl.BlockSpec(memory_space=pltpu.VMEM)
HBM = pl.BlockSpec(memory_space=pltpu.HBM)
SMEM = pl.BlockSpec(memory_space=pltpu.SMEM)
F32, BF16 = jnp.float32, jnp.bfloat16
STEP = 8
GRADS = HID + 16
PACK = TGT + 16
Z_GROUPS = [[y * NZ + z for z in range(NZ)] for y in range(NY)]
X_GROUPS = [[x * NCORE + core for x in range(NX)] for core in range(NCORE)]


def call(kernel, outs, ins, scratch=(), flops=0, moved=0, limit=16):
    return pl.pallas_call(
        kernel,
        out_shape=outs,
        in_specs=ins,
        out_specs=[VMEM] * len(outs),
        scratch_shapes=list(scratch),
        compiler_params=pltpu.CompilerParams(vmem_limit_bytes=limit * 1024 * 1024),
        cost_estimate=pl.CostEstimate(flops=flops, bytes_accessed=moved, transcendentals=0),
    )


def sds(shape, dtype):
    return jax.ShapeDtypeStruct(shape, dtype)


def exchange_dom(value, distance):
    pairs = [(i, i ^ distance) for i in range(DOM)]
    return lax.ppermute(value, "dom", pairs)


def swap(value, axis, groups=None):
    return lax.all_to_all(value, axis, 0, 0, axis_index_groups=groups, tiled=True)


def stream(ids, mask, numbers, staged, mask_sems, id_sem):
    def mask_copy(i):
        at = pl.ds(i * STEP, STEP)
        return pltpu.make_async_copy(mask.at[at], staged.at[at], mask_sems.at[i])

    id_copy = pltpu.make_async_copy(ids, numbers, id_sem.at[0])
    id_copy.start()
    for i in range(mask.shape[0] // STEP):
        mask_copy(i).start()
    return id_copy.wait, lambda i: mask_copy(i).wait()


def stream_scratch(tile_mask):
    return [
        pltpu.SMEM((tile_mask.shape[0],), jnp.int32),
        pltpu.VMEM(tile_mask.shape, jnp.int32),
        pltpu.SemaphoreType.DMA((tile_mask.shape[0] // STEP,)),
        pltpu.SemaphoreType.DMA((1,)),
    ]


def forward_kernel(ids, mask, *refs):
    pieces, outs = refs[:DOM], refs[DOM : DOM + 7]
    sources, totals, numbers, staged, mask_sems, id_sem = refs[DOM + 7 :]
    wait_numbers, wait_tiles = stream(ids, mask, numbers, staged, mask_sems, id_sem)
    my_dom = lax.axis_index("dom")
    for k in range(DOM):
        at = my_dom ^ k
        sources[2 * at] = pieces[k][0:BLK, :]
        sources[2 * at + 1] = pieces[k][BLK:, :]
    totals[...] = jnp.zeros_like(totals)
    wait_numbers()

    def step(i, carry):
        wait_tiles(i)
        for u in range(STEP):
            t = i * STEP + u
            r, c = numbers[t] >> 4, numbers[t] & 15
            tile = staged[t].astype(F32).astype(BF16)
            totals[r] = totals[r] + jnp.dot(tile, sources[c], preferred_element_type=F32)
        return carry

    lax.fori_loop(0, mask.shape[0] // STEP, step, 0)
    y = lax.axis_index("col") >> 3
    half = NZ // 2
    own, far_up, far_down, up_low, up_high, down_low, down_high = outs
    for out, step_to, first, count in (
        (far_up, 2, 0, half),
        (far_down, 2, half, half),
        (up_high, 1, half, half),
        (down_low, 3, 0, half),
        (up_low, 1, 0, half),
        (down_high, 3, half, half),
        (own, 0, 0, NZ),
    ):
        for z in range(count):
            out[z] = totals[((y + step_to) & 3) * NZ + first + z].astype(BF16)


def forward(ids, tile_mask, pieces):
    tiles = tile_mask.shape[0]
    return pl.pallas_call(
        forward_kernel,
        out_shape=[sds((NZ, BLK, F), BF16)] + [sds((NZ // 2, BLK, F), BF16)] * 6,
        in_specs=[HBM, HBM] + [VMEM] * DOM,
        out_specs=[VMEM] * 7,
        scratch_shapes=[
            pltpu.VMEM((DOM * 2, BLK, F), BF16),
            pltpu.VMEM((COL, BLK, F), F32),
        ]
        + stream_scratch(tile_mask),
        compiler_params=pltpu.CompilerParams(vmem_limit_bytes=52 * 1024 * 1024),
        cost_estimate=pl.CostEstimate(
            flops=2 * tiles * BLK**3, bytes_accessed=tiles * BLK * BLK * 4, transcendentals=0
        ),
    )(ids, tile_mask, *pieces)


def column(row):
    return jnp.transpose(jnp.broadcast_to(row, (BLK, BLK)))


def sigmoid(v):
    return 1.0 / (1.0 + jnp.exp(-v))


def relay_kernel(up, far_up, down, far_down, out_up, out_down):
    for z in range(NZ // 2):
        out_up[z] = (up[z].astype(F32) + far_up[z].astype(F32)).astype(BF16)
        out_down[z] = (down[z].astype(F32) + far_down[z].astype(F32)).astype(BF16)


def y_sum_kernel(own, low_above, low_below, high_below, high_above, out):
    half = NZ // 2
    for z in range(half):
        low = low_above[z].astype(F32) + low_below[z].astype(F32)
        out[z] = (own[z].astype(F32) + low).astype(BF16)
        high = high_below[z].astype(F32) + high_above[z].astype(F32)
        out[z + half] = (own[z + half].astype(F32) + high).astype(BF16)


def step_y(value, step):
    pairs = [(i, ((i // NZ + step) % NY) * NZ + i % NZ) for i in range(COL)]
    return lax.ppermute(value, "col", pairs)


def dense_kernel(parts, dest_scale, weight, bias, targets, upstream, hidden, packed):
    summed = parts[0].astype(F32)
    for z in range(1, NZ):
        summed = summed + parts[z].astype(F32)
    scale = column(dest_scale[...])
    aggregated = (summed * scale).astype(BF16)
    w = weight[...]
    preact = jnp.dot(aggregated, w, preferred_element_type=F32) + bias[...]
    hidden[...] = (preact * sigmoid(preact)).astype(BF16)
    wanted = targets[...]
    row_ids = lax.broadcasted_iota(jnp.int32, (BLK, TGT), 0)
    chosen = (row_ids == wanted).astype(F32)
    chosen_b = chosen.astype(BF16)
    agg_t = lax.dot_general(
        chosen_b, aggregated, (((0,), (0,)), ((), ())), preferred_element_type=F32
    ).astype(BF16)
    pre_t = jnp.dot(agg_t, w, preferred_element_type=F32) + bias[...]
    s = sigmoid(pre_t)
    slope = (upstream[...].astype(F32) * (s * (1.0 + pre_t * (1.0 - s)))).astype(BF16)
    weight_part = lax.dot_general(
        agg_t, slope, (((0,), (0,)), ((), ())), preferred_element_type=F32
    )
    bias_part = jnp.sum(slope.astype(F32), axis=0, keepdims=True)
    term = lax.dot_general(
        slope, w, (((1,), (1,)), ((), ())), preferred_element_type=F32
    )
    same = lax.dot_general(
        chosen_b, chosen_b, (((0,), (0,)), ((), ())), preferred_element_type=F32
    )
    collected = jnp.dot(
        same, term, preferred_element_type=F32, precision=lax.Precision.HIGHEST
    )
    scale_t = lax.dot_general(
        chosen, scale, (((0,), (0,)), ((), ())), preferred_element_type=F32,
        precision=lax.Precision.HIGHEST,
    )
    k_row = lax.broadcasted_iota(jnp.int32, (TGT, TGT), 0)
    k_col = lax.broadcasted_iota(jnp.int32, (TGT, TGT), 1)
    earlier = jnp.sum(jnp.where(k_col < k_row, same, 0.0), axis=1, keepdims=True)
    returned = jnp.where(earlier > 0.0, 0.0, collected * scale_t).astype(BF16)
    names = jnp.concatenate([wanted.astype(F32)] * (BLK // TGT), axis=1)
    lanes = lax.broadcasted_iota(jnp.int32, (1, BLK), 1)
    names = jnp.where(lanes // TGT == (lax.axis_index("col") & 3), names, -1.0)
    high = bias_part.astype(BF16).astype(F32)
    low = bias_part - high
    sundry = jnp.concatenate(
        [names, high[:, :BLK], high[:, BLK:], low[:, :BLK], low[:, BLK:], jnp.zeros((3, BLK), F32)],
        axis=0,
    )
    for c in range(COL):
        at, side = 8 * (c // 2), BLK * (c % 2)
        chunk = weight_part[at : at + 8, side : side + BLK]
        packed[c, 0:TGT, :] = returned
        packed[c, TGT:, :] = jnp.concatenate([chunk, sundry], axis=0).astype(BF16)


def gradient_kernel(packed, chunks, bias):
    total = packed[0, TGT:, :].astype(F32)
    for c in range(1, COL):
        total = total + packed[c, TGT:, :].astype(F32)
    for c in range(COL):
        chunks[c] = total[0:8, :]
    bias[...] = jnp.concatenate([total[9:10] + total[11:12], total[10:11] + total[12:13]], axis=1)


def unpack(packed, returned):
    row_ids = lax.broadcasted_iota(jnp.int32, (BLK, BLK), 0).astype(F32)
    quarters = BLK // TGT
    for g in range(COL // quarters):
        held = slice(g * quarters, (g + 1) * quarters)
        rows = jnp.transpose(packed[held, 0:TGT, :].reshape(BLK, F))
        for first in range(g * quarters, (g + 1) * quarters, 2):
            chosen = [
                (row_ids == packed[c, TGT:, :].astype(F32)[8:9, :]).astype(BF16)
                for c in (first, first + 1)
            ]
            placed = lax.dot_general(
                rows,
                jnp.concatenate(chosen, axis=0),
                (((1,), (1,)), ((), ())),
                preferred_element_type=F32,
            ).astype(BF16)
            returned[first] = placed[:, :BLK]
            returned[first + 1] = placed[:, BLK:]


def bias_rows(bias):
    high = bias.astype(BF16).astype(F32)
    low = bias - high
    return jnp.concatenate(
        [high[:, :BLK], high[:, BLK:], low[:, :BLK], low[:, BLK:], jnp.zeros((12, BLK), F32)],
        axis=0,
    ).astype(BF16)


def bias_of(rows):
    rows = rows.astype(F32)
    return jnp.concatenate([rows[0:1] + rows[2:3], rows[1:2] + rows[3:4]], axis=1)


def backward_kernel(ids, mask, packed, bias, own, other, returned, totals, *work):
    numbers, staged = work[:2]
    wait_numbers, wait_tiles = stream(ids, mask, *work)
    my_core = lax.axis_index("dom") & 1
    for ref in (own, other):
        ref[NX * 256 :, :] = bias_rows(bias[...])
    unpack(packed, returned)
    totals[...] = jnp.zeros_like(totals)
    wait_numbers()

    def step(i, carry):
        wait_tiles(i)
        for u in range(STEP):
            t = i * STEP + u
            r, c = numbers[t] >> 4, numbers[t] & 15
            tile = staged[t].astype(F32).astype(BF16)
            totals[c] = totals[c] + jnp.dot(returned[r], tile, preferred_element_type=F32)
        return carry

    lax.fori_loop(0, mask.shape[0] // STEP, step, 0)
    for x in range(NX):
        for half in range(2):
            rows_at = pl.ds(x * 256 + half * BLK, BLK)
            for ref, core in ((own, my_core), (other, 1 - my_core)):
                block = (x * NCORE + core) * 2 + half
                ref[rows_at, :] = jnp.transpose(totals[block]).astype(BF16)


def core_sum_kernel(own, got, grads, grads_got, out):
    at = NX * 256
    bias = bias_rows(bias_of(own[at:, :]) + bias_of(got[at:, :]))
    weight_sum = [(grads[c] + grads_got[c]).astype(BF16) for c in range(COL)]
    for x in range(NX):
        rows_at = slice(x * 256, (x + 1) * 256)
        total = own[rows_at, :].astype(F32) + got[rows_at, :].astype(F32)
        out[x, 0:256, :] = total.astype(BF16)
        for c in range(0, COL, 2):
            out[x, 256 + 8 * c : 272 + 8 * c, :] = jnp.concatenate(weight_sum[c : c + 2], axis=0)
        out[x, 256 + HID :, :] = bias


def finish_kernel(parts, source_scale, grad, weight_grad, bias_grad):
    def total(at):
        return (parts[0, at, :].astype(F32) + parts[1, at, :].astype(F32)) + (
            parts[2, at, :].astype(F32) + parts[3, at, :].astype(F32)
        )

    for half in range(2):
        at = slice(half * BLK, (half + 1) * BLK)
        grad[at, :] = total(at) * column(source_scale[:, at])
    for c in range(0, COL, 2):
        both = total(slice(256 + 8 * c, 272 + 8 * c))
        rows_at = slice(4 * c, 4 * c + 8)
        weight_grad[rows_at, :BLK] = both[0:8]
        weight_grad[rows_at, BLK:] = both[8:16]
    bias = [bias_of(parts[x, 256 + HID :, :]) for x in range(NX)]
    bias_grad[...] = (bias[0] + bias[1]) + (bias[2] + bias[3])


def body(
    source_feats,
    source_scale,
    dest_scale,
    weight,
    layer_bias,
    tile_rows,
    tile_cols,
    tile_mask,
    targets,
    upstream,
):
    scaled = (source_feats.astype(F32) * source_scale[:, None]).astype(BF16)
    along_x = [scaled] + [exchange_dom(scaled, NCORE * k) for k in range(1, NX)]
    pieces = [piece for held in along_x for piece in (held, exchange_dom(held, 1))]
    products = 2 * tile_mask.shape[0] * BLK**3
    ids = tile_rows * 16 + tile_cols
    own, far_up, far_down, up_low, up_high, down_low, down_high = forward(ids, tile_mask, pieces)
    far_up, far_down = step_y(far_up, 1), step_y(far_down, -1)
    high_below, low_above = step_y(up_high, 1), step_y(down_low, -1)
    up, down = call(relay_kernel, [sds((NZ // 2, BLK, F), BF16)] * 2, [VMEM] * 4)(
        up_low, far_up, down_high, far_down
    )
    low_below, high_above = step_y(up, 1), step_y(down, -1)
    (line,) = call(y_sum_kernel, [sds((NZ, BLK, F), BF16)], [VMEM] * 5)(
        own, low_above, low_below, high_below, high_above
    )
    parts = swap(line, "col", Z_GROUPS)
    hidden, packed = call(
        dense_kernel,
        [sds((BLK, HID), BF16), sds((COL, PACK, F), BF16)],
        [VMEM] * 6,
    )(
        parts,
        dest_scale.reshape(1, BLK),
        weight,
        layer_bias.reshape(1, HID),
        targets.reshape(1, TGT),
        upstream,
    )
    gathered = swap(packed, "col")
    chunks, bias_sum = call(
        gradient_kernel, [sds((COL, 8, BLK), F32), sds((1, HID), F32)], [VMEM]
    )(gathered)
    grads = swap(chunks, "col")
    own, other = call(
        backward_kernel,
        [sds((NX * 256 + 16, F), BF16)] * 2,
        [HBM, HBM, VMEM, VMEM],
        [pltpu.VMEM((COL, F, BLK), BF16), pltpu.VMEM((DOM * 2, F, BLK), F32)]
        + stream_scratch(tile_mask),
        flops=products,
        limit=52,
    )(ids, tile_mask, gathered, bias_sum)
    got = exchange_dom(other, 1)
    grads_got = exchange_dom(grads, 1)
    (by_x,) = call(core_sum_kernel, [sds((NX, 256 + GRADS, F), BF16)], [VMEM] * 4)(
        own, got, grads, grads_got
    )
    input_grad, weight_grad, bias_grad = call(
        finish_kernel,
        [sds((256, F), F32), sds((F, HID), F32), sds((1, HID), F32)],
        [VMEM] * 2,
    )(swap(by_x, "dom", X_GROUPS), source_scale.reshape(1, 256))
    return hidden, weight_grad, bias_grad.reshape(HID), input_grad


def solution(mesh):
    placed = (
        P(("col", "dom"), None),
        P(("col", "dom")),
        P(("col", "dom")),
        P(),
        P(),
        P(("col", "dom")),
        P(("col", "dom")),
        P(("col", "dom"), None, None),
        P(("col", "dom")),
        P(("col", "dom"), None),
    )
    return jax.shard_map(
        body,
        mesh=mesh,
        in_specs=placed,
        out_specs=(P(("col", "dom"), None), P(), P(), P(("col", "dom"), None)),
        check_vma=False,
    )
```

```python
import jax
import jax.numpy as jnp
from jax import lax
from jax.experimental import pallas as pl
from jax.experimental.pallas import tpu as pltpu
from jax.sharding import PartitionSpec as P

NY, NZ, NX, NCORE = 4, 8, 4, 2
COL, DOM = NY * NZ, NX * NCORE
BLK = 128
F = 128
HID = 256
TGT = 32
VMEM = pl.BlockSpec(memory_space=pltpu.VMEM)
HBM = pl.BlockSpec(memory_space=pltpu.HBM)
SMEM = pl.BlockSpec(memory_space=pltpu.SMEM)
F32, BF16 = jnp.float32, jnp.bfloat16
STEP = 16
GRADS = HID + 16
PACK = TGT + 16
Z_GROUPS = [[y * NZ + z for z in range(NZ)] for y in range(NY)]
X_GROUPS = [[x * NCORE + core for x in range(NX)] for core in range(NCORE)]


def call(kernel, outs, ins, scratch=(), flops=0, moved=0, limit=16):
    return pl.pallas_call(
        kernel,
        out_shape=outs,
        in_specs=ins,
        out_specs=[VMEM] * len(outs),
        scratch_shapes=list(scratch),
        compiler_params=pltpu.CompilerParams(vmem_limit_bytes=limit * 1024 * 1024),
        cost_estimate=pl.CostEstimate(flops=flops, bytes_accessed=moved, transcendentals=0),
    )


def sds(shape, dtype):
    return jax.ShapeDtypeStruct(shape, dtype)


def exchange_dom(value, distance):
    pairs = [(i, i ^ distance) for i in range(DOM)]
    return lax.ppermute(value, "dom", pairs)


def swap(value, axis, groups=None):
    return lax.all_to_all(value, axis, 0, 0, axis_index_groups=groups, tiled=True)


def stream(ids, mask, numbers, staged, mask_sems, id_sem):
    def mask_copy(i):
        at = pl.ds(i * STEP, STEP)
        return pltpu.make_async_copy(mask.at[at], staged.at[at], mask_sems.at[i])

    id_copy = pltpu.make_async_copy(ids, numbers, id_sem.at[0])
    id_copy.start()
    for i in range(mask.shape[0] // STEP):
        mask_copy(i).start()
    return id_copy.wait, lambda i: mask_copy(i).wait()


def stream_scratch(tile_mask):
    return [
        pltpu.SMEM((tile_mask.shape[0],), jnp.int32),
        pltpu.VMEM(tile_mask.shape, jnp.int32),
        pltpu.SemaphoreType.DMA((tile_mask.shape[0] // STEP,)),
        pltpu.SemaphoreType.DMA((1,)),
    ]


def forward_kernel(ids, mask, *refs):
    pieces, outs = refs[:DOM], refs[DOM : DOM + 7]
    sources, totals, numbers, staged, mask_sems, id_sem = refs[DOM + 7 :]
    wait_numbers, wait_tiles = stream(ids, mask, numbers, staged, mask_sems, id_sem)
    my_dom = lax.axis_index("dom")
    for k in range(DOM):
        at = my_dom ^ k
        sources[2 * at] = pieces[k][0:BLK, :]
        sources[2 * at + 1] = pieces[k][BLK:, :]
    totals[...] = jnp.zeros_like(totals)
    wait_numbers()

    def step(i, carry):
        wait_tiles(i)
        for u in range(STEP):
            t = i * STEP + u
            r, c = numbers[t] >> 4, numbers[t] & 15
            tile = staged[t].astype(F32).astype(BF16)
            totals[r] = totals[r] + jnp.dot(tile, sources[c], preferred_element_type=F32)
        return carry

    lax.fori_loop(0, mask.shape[0] // STEP, step, 0)
    y = lax.axis_index("col") >> 3
    half = NZ // 2
    own, far_up, far_down, up_low, up_high, down_low, down_high = outs
    for out, step_to, first, count in (
        (far_up, 2, 0, half),
        (far_down, 2, half, half),
        (up_high, 1, half, half),
        (down_low, 3, 0, half),
        (up_low, 1, 0, half),
        (down_high, 3, half, half),
        (own, 0, 0, NZ),
    ):
        for z in range(count):
            out[z] = totals[((y + step_to) & 3) * NZ + first + z].astype(BF16)


def forward(ids, tile_mask, pieces):
    tiles = tile_mask.shape[0]
    return pl.pallas_call(
        forward_kernel,
        out_shape=[sds((NZ, BLK, F), BF16)] + [sds((NZ // 2, BLK, F), BF16)] * 6,
        in_specs=[HBM, HBM] + [VMEM] * DOM,
        out_specs=[VMEM] * 7,
        scratch_shapes=[
            pltpu.VMEM((DOM * 2, BLK, F), BF16),
            pltpu.VMEM((COL, BLK, F), F32),
        ]
        + stream_scratch(tile_mask),
        compiler_params=pltpu.CompilerParams(vmem_limit_bytes=52 * 1024 * 1024),
        cost_estimate=pl.CostEstimate(
            flops=2 * tiles * BLK**3, bytes_accessed=tiles * BLK * BLK * 4, transcendentals=0
        ),
    )(ids, tile_mask, *pieces)


def column(row):
    return jnp.transpose(jnp.broadcast_to(row, (BLK, BLK)))


def sigmoid(v):
    return 1.0 / (1.0 + jnp.exp(-v))


def relay_kernel(up, far_up, down, far_down, out_up, out_down):
    for z in range(NZ // 2):
        out_up[z] = (up[z].astype(F32) + far_up[z].astype(F32)).astype(BF16)
        out_down[z] = (down[z].astype(F32) + far_down[z].astype(F32)).astype(BF16)


def y_sum_kernel(own, low_above, low_below, high_below, high_above, out):
    half = NZ // 2
    for z in range(half):
        low = low_above[z].astype(F32) + low_below[z].astype(F32)
        out[z] = (own[z].astype(F32) + low).astype(BF16)
        high = high_below[z].astype(F32) + high_above[z].astype(F32)
        out[z + half] = (own[z + half].astype(F32) + high).astype(BF16)


def step_y(value, step):
    pairs = [(i, ((i // NZ + step) % NY) * NZ + i % NZ) for i in range(COL)]
    return lax.ppermute(value, "col", pairs)


def dense_kernel(parts, dest_scale, weight, bias, targets, upstream, hidden, packed):
    summed = parts[0].astype(F32)
    for z in range(1, NZ):
        summed = summed + parts[z].astype(F32)
    scale = column(dest_scale[...])
    aggregated = (summed * scale).astype(BF16)
    w = weight[...]
    preact = jnp.dot(aggregated, w, preferred_element_type=F32) + bias[...]
    hidden[...] = (preact * sigmoid(preact)).astype(BF16)
    wanted = targets[...]
    row_ids = lax.broadcasted_iota(jnp.int32, (BLK, TGT), 0)
    chosen = (row_ids == wanted).astype(F32)
    chosen_b = chosen.astype(BF16)
    agg_t = lax.dot_general(
        chosen_b, aggregated, (((0,), (0,)), ((), ())), preferred_element_type=F32
    ).astype(BF16)
    pre_t = jnp.dot(agg_t, w, preferred_element_type=F32) + bias[...]
    s = sigmoid(pre_t)
    slope = (upstream[...].astype(F32) * (s * (1.0 + pre_t * (1.0 - s)))).astype(BF16)
    weight_part = lax.dot_general(
        agg_t, slope, (((0,), (0,)), ((), ())), preferred_element_type=F32
    )
    bias_part = jnp.sum(slope.astype(F32), axis=0, keepdims=True)
    term = lax.dot_general(
        slope, w, (((1,), (1,)), ((), ())), preferred_element_type=F32
    )
    same = lax.dot_general(
        chosen_b, chosen_b, (((0,), (0,)), ((), ())), preferred_element_type=F32
    )
    collected = jnp.dot(
        same, term, preferred_element_type=F32, precision=lax.Precision.HIGHEST
    )
    scale_t = lax.dot_general(
        chosen, scale, (((0,), (0,)), ((), ())), preferred_element_type=F32,
        precision=lax.Precision.HIGHEST,
    )
    k_row = lax.broadcasted_iota(jnp.int32, (TGT, TGT), 0)
    k_col = lax.broadcasted_iota(jnp.int32, (TGT, TGT), 1)
    earlier = jnp.sum(jnp.where(k_col < k_row, same, 0.0), axis=1, keepdims=True)
    returned = jnp.where(earlier > 0.0, 0.0, collected * scale_t).astype(BF16)
    names = jnp.concatenate([wanted.astype(F32)] * (BLK // TGT), axis=1)
    lanes = lax.broadcasted_iota(jnp.int32, (1, BLK), 1)
    names = jnp.where(lanes // TGT == (lax.axis_index("col") & 3), names, -1.0)
    high = bias_part.astype(BF16).astype(F32)
    low = bias_part - high
    sundry = jnp.concatenate(
        [names, high[:, :BLK], high[:, BLK:], low[:, :BLK], low[:, BLK:], jnp.zeros((3, BLK), F32)],
        axis=0,
    )
    for c in range(COL):
        at, side = 8 * (c // 2), BLK * (c % 2)
        chunk = weight_part[at : at + 8, side : side + BLK]
        packed[c, 0:TGT, :] = returned
        packed[c, TGT:, :] = jnp.concatenate([chunk, sundry], axis=0).astype(BF16)


def gradient_kernel(packed, chunks, bias):
    total = packed[0, TGT:, :].astype(F32)
    for c in range(1, COL):
        total = total + packed[c, TGT:, :].astype(F32)
    for c in range(COL):
        chunks[c] = total[0:8, :]
    bias[...] = jnp.concatenate([total[9:10] + total[11:12], total[10:11] + total[12:13]], axis=1)


def unpack(packed, returned):
    row_ids = lax.broadcasted_iota(jnp.int32, (BLK, BLK), 0).astype(F32)
    quarters = BLK // TGT
    for g in range(COL // quarters):
        held = slice(g * quarters, (g + 1) * quarters)
        rows = jnp.transpose(packed[held, 0:TGT, :].reshape(BLK, F))
        for first in range(g * quarters, (g + 1) * quarters, 2):
            chosen = [
                (row_ids == packed[c, TGT:, :].astype(F32)[8:9, :]).astype(BF16)
                for c in (first, first + 1)
            ]
            placed = lax.dot_general(
                rows,
                jnp.concatenate(chosen, axis=0),
                (((1,), (1,)), ((), ())),
                preferred_element_type=F32,
            ).astype(BF16)
            returned[first] = placed[:, :BLK]
            returned[first + 1] = placed[:, BLK:]


def bias_rows(bias):
    high = bias.astype(BF16).astype(F32)
    low = bias - high
    return jnp.concatenate(
        [high[:, :BLK], high[:, BLK:], low[:, :BLK], low[:, BLK:], jnp.zeros((12, BLK), F32)],
        axis=0,
    ).astype(BF16)


def bias_of(rows):
    rows = rows.astype(F32)
    return jnp.concatenate([rows[0:1] + rows[2:3], rows[1:2] + rows[3:4]], axis=1)


def backward_kernel(ids, mask, packed, bias, own, other, returned, totals, *work):
    numbers, staged = work[:2]
    wait_numbers, wait_tiles = stream(ids, mask, *work)
    my_core = lax.axis_index("dom") & 1
    for ref in (own, other):
        ref[NX * 256 :, :] = bias_rows(bias[...])
    unpack(packed, returned)
    totals[...] = jnp.zeros_like(totals)
    wait_numbers()

    def step(i, carry):
        wait_tiles(i)
        for u in range(STEP):
            t = i * STEP + u
            r, c = numbers[t] >> 4, numbers[t] & 15
            tile = staged[t].astype(F32).astype(BF16)
            totals[c] = totals[c] + jnp.dot(returned[r], tile, preferred_element_type=F32)
        return carry

    lax.fori_loop(0, mask.shape[0] // STEP, step, 0)
    for x in range(NX):
        for half in range(2):
            rows_at = pl.ds(x * 256 + half * BLK, BLK)
            for ref, core in ((own, my_core), (other, 1 - my_core)):
                block = (x * NCORE + core) * 2 + half
                ref[rows_at, :] = jnp.transpose(totals[block]).astype(BF16)


def core_sum_kernel(own, got, grads, grads_got, out):
    at = NX * 256
    bias = bias_rows(bias_of(own[at:, :]) + bias_of(got[at:, :]))
    weight_sum = [(grads[c] + grads_got[c]).astype(BF16) for c in range(COL)]
    for x in range(NX):
        rows_at = slice(x * 256, (x + 1) * 256)
        total = own[rows_at, :].astype(F32) + got[rows_at, :].astype(F32)
        out[x, 0:256, :] = total.astype(BF16)
        for c in range(0, COL, 2):
            out[x, 256 + 8 * c : 272 + 8 * c, :] = jnp.concatenate(weight_sum[c : c + 2], axis=0)
        out[x, 256 + HID :, :] = bias


def finish_kernel(parts, source_scale, grad, weight_grad, bias_grad):
    def total(at):
        return (parts[0, at, :].astype(F32) + parts[1, at, :].astype(F32)) + (
            parts[2, at, :].astype(F32) + parts[3, at, :].astype(F32)
        )

    for half in range(2):
        at = slice(half * BLK, (half + 1) * BLK)
        grad[at, :] = total(at) * column(source_scale[:, at])
    for c in range(0, COL, 2):
        both = total(slice(256 + 8 * c, 272 + 8 * c))
        rows_at = slice(4 * c, 4 * c + 8)
        weight_grad[rows_at, :BLK] = both[0:8]
        weight_grad[rows_at, BLK:] = both[8:16]
    bias = [bias_of(parts[x, 256 + HID :, :]) for x in range(NX)]
    bias_grad[...] = (bias[0] + bias[1]) + (bias[2] + bias[3])


def body(
    source_feats,
    source_scale,
    dest_scale,
    weight,
    layer_bias,
    tile_rows,
    tile_cols,
    tile_mask,
    targets,
    upstream,
):
    scaled = (source_feats.astype(F32) * source_scale[:, None]).astype(BF16)
    along_x = [scaled] + [exchange_dom(scaled, NCORE * k) for k in range(1, NX)]
    pieces = [piece for held in along_x for piece in (held, exchange_dom(held, 1))]
    products = 2 * tile_mask.shape[0] * BLK**3
    ids = tile_rows * 16 + tile_cols
    own, far_up, far_down, up_low, up_high, down_low, down_high = forward(ids, tile_mask, pieces)
    far_up, far_down = step_y(far_up, 1), step_y(far_down, -1)
    high_below, low_above = step_y(up_high, 1), step_y(down_low, -1)
    up, down = call(relay_kernel, [sds((NZ // 2, BLK, F), BF16)] * 2, [VMEM] * 4)(
        up_low, far_up, down_high, far_down
    )
    low_below, high_above = step_y(up, 1), step_y(down, -1)
    (line,) = call(y_sum_kernel, [sds((NZ, BLK, F), BF16)], [VMEM] * 5)(
        own, low_above, low_below, high_below, high_above
    )
    parts = swap(line, "col", Z_GROUPS)
    hidden, packed = call(
        dense_kernel,
        [sds((BLK, HID), BF16), sds((COL, PACK, F), BF16)],
        [VMEM] * 6,
    )(
        parts,
        dest_scale.reshape(1, BLK),
        weight,
        layer_bias.reshape(1, HID),
        targets.reshape(1, TGT),
        upstream,
    )
    gathered = swap(packed, "col")
    chunks, bias_sum = call(
        gradient_kernel, [sds((COL, 8, BLK), F32), sds((1, HID), F32)], [VMEM]
    )(gathered)
    grads = swap(chunks, "col")
    own, other = call(
        backward_kernel,
        [sds((NX * 256 + 16, F), BF16)] * 2,
        [HBM, HBM, VMEM, VMEM],
        [pltpu.VMEM((COL, F, BLK), BF16), pltpu.VMEM((DOM * 2, F, BLK), F32)]
        + stream_scratch(tile_mask),
        flops=products,
        limit=52,
    )(ids, tile_mask, gathered, bias_sum)
    got = exchange_dom(other, 1)
    grads_got = exchange_dom(grads, 1)
    (by_x,) = call(core_sum_kernel, [sds((NX, 256 + GRADS, F), BF16)], [VMEM] * 4)(
        own, got, grads, grads_got
    )
    input_grad, weight_grad, bias_grad = call(
        finish_kernel,
        [sds((256, F), F32), sds((F, HID), F32), sds((1, HID), F32)],
        [VMEM] * 2,
    )(swap(by_x, "dom", X_GROUPS), source_scale.reshape(1, 256))
    return hidden, weight_grad, bias_grad.reshape(HID), input_grad


def solution(mesh):
    placed = (
        P(("col", "dom"), None),
        P(("col", "dom")),
        P(("col", "dom")),
        P(),
        P(),
        P(("col", "dom")),
        P(("col", "dom")),
        P(("col", "dom"), None, None),
        P(("col", "dom")),
        P(("col", "dom"), None),
    )
    return jax.shard_map(
        body,
        mesh=mesh,
        in_specs=placed,
        out_specs=(P(("col", "dom"), None), P(), P(), P(("col", "dom"), None)),
        check_vma=False,
    )
```

```python
import jax
import jax.numpy as jnp
from jax import lax
from jax.experimental import pallas as pl
from jax.experimental.pallas import tpu as pltpu
from jax.sharding import PartitionSpec as P

NY, NZ, NX, NCORE = 4, 8, 4, 2
COL, DOM = NY * NZ, NX * NCORE
BLK = 128
F = 128
HID = 256
TGT = 32
VMEM = pl.BlockSpec(memory_space=pltpu.VMEM)
HBM = pl.BlockSpec(memory_space=pltpu.HBM)
SMEM = pl.BlockSpec(memory_space=pltpu.SMEM)
F32, BF16 = jnp.float32, jnp.bfloat16
STEP = 16
GRADS = HID + 16
PACK = TGT + 16
Z_GROUPS = [[y * NZ + z for z in range(NZ)] for y in range(NY)]
X_GROUPS = [[x * NCORE + core for x in range(NX)] for core in range(NCORE)]


def call(kernel, outs, ins, scratch=(), flops=0, moved=0, limit=16):
    return pl.pallas_call(
        kernel,
        out_shape=outs,
        in_specs=ins,
        out_specs=[VMEM] * len(outs),
        scratch_shapes=list(scratch),
        compiler_params=pltpu.CompilerParams(vmem_limit_bytes=limit * 1024 * 1024),
        cost_estimate=pl.CostEstimate(flops=flops, bytes_accessed=moved, transcendentals=0),
    )


def sds(shape, dtype):
    return jax.ShapeDtypeStruct(shape, dtype)


def exchange_dom(value, distance):
    pairs = [(i, i ^ distance) for i in range(DOM)]
    return lax.ppermute(value, "dom", pairs)


def swap(value, axis, groups=None):
    return lax.all_to_all(value, axis, 0, 0, axis_index_groups=groups, tiled=True)


def stream(ids, mask, numbers, staged, mask_sems, id_sem):
    def mask_copy(i):
        at = pl.ds(i * STEP, STEP)
        return pltpu.make_async_copy(mask.at[at], staged.at[at], mask_sems.at[i])

    id_copy = pltpu.make_async_copy(ids, numbers, id_sem.at[0])
    id_copy.start()
    for i in range(mask.shape[0] // STEP):
        mask_copy(i).start()
    return id_copy.wait, lambda i: mask_copy(i).wait()


def stream_scratch(tile_mask):
    return [
        pltpu.SMEM((tile_mask.shape[0],), jnp.int32),
        pltpu.VMEM(tile_mask.shape, jnp.int32),
        pltpu.SemaphoreType.DMA((tile_mask.shape[0] // STEP,)),
        pltpu.SemaphoreType.DMA((1,)),
    ]


def forward_kernel(ids, mask, *refs):
    pieces, outs = refs[:DOM], refs[DOM : DOM + 7]
    sources, totals, numbers, staged, mask_sems, id_sem = refs[DOM + 7 :]
    wait_numbers, wait_tiles = stream(ids, mask, numbers, staged, mask_sems, id_sem)
    my_dom = lax.axis_index("dom")
    for k in range(DOM):
        at = my_dom ^ k
        sources[2 * at] = pieces[k][0:BLK, :]
        sources[2 * at + 1] = pieces[k][BLK:, :]
    totals[...] = jnp.zeros_like(totals)
    wait_numbers()

    def step(i, carry):
        wait_tiles(i)
        for u in range(STEP):
            t = i * STEP + u
            r, c = numbers[t] >> 4, numbers[t] & 15
            tile = staged[t].astype(F32).astype(BF16)
            totals[r] = totals[r] + jnp.dot(tile, sources[c], preferred_element_type=F32)
        return carry

    lax.fori_loop(0, mask.shape[0] // STEP, step, 0)
    y = lax.axis_index("col") >> 3
    half = NZ // 2
    own, far_up, far_down, up_low, up_high, down_low, down_high = outs
    for out, step_to, first, count in (
        (far_up, 2, 0, half),
        (far_down, 2, half, half),
        (up_high, 1, half, half),
        (down_low, 3, 0, half),
        (up_low, 1, 0, half),
        (down_high, 3, half, half),
        (own, 0, 0, NZ),
    ):
        for z in range(count):
            out[z] = totals[((y + step_to) & 3) * NZ + first + z].astype(BF16)


def forward(ids, tile_mask, pieces):
    tiles = tile_mask.shape[0]
    return pl.pallas_call(
        forward_kernel,
        out_shape=[sds((NZ, BLK, F), BF16)] + [sds((NZ // 2, BLK, F), BF16)] * 6,
        in_specs=[HBM, HBM] + [VMEM] * DOM,
        out_specs=[VMEM] * 7,
        scratch_shapes=[
            pltpu.VMEM((DOM * 2, BLK, F), BF16),
            pltpu.VMEM((COL, BLK, F), F32),
        ]
        + stream_scratch(tile_mask),
        compiler_params=pltpu.CompilerParams(vmem_limit_bytes=52 * 1024 * 1024),
        cost_estimate=pl.CostEstimate(
            flops=2 * tiles * BLK**3, bytes_accessed=tiles * BLK * BLK * 4, transcendentals=0
        ),
    )(ids, tile_mask, *pieces)


def column(row):
    return jnp.transpose(jnp.broadcast_to(row, (BLK, BLK)))


def sigmoid(v):
    return 1.0 / (1.0 + jnp.exp(-v))


def relay_kernel(up, far_up, down, far_down, out_up, out_down):
    for z in range(NZ // 2):
        out_up[z] = (up[z].astype(F32) + far_up[z].astype(F32)).astype(BF16)
        out_down[z] = (down[z].astype(F32) + far_down[z].astype(F32)).astype(BF16)


def y_sum_kernel(own, low_above, low_below, high_below, high_above, out):
    half = NZ // 2
    for z in range(half):
        low = low_above[z].astype(F32) + low_below[z].astype(F32)
        out[z] = (own[z].astype(F32) + low).astype(BF16)
        high = high_below[z].astype(F32) + high_above[z].astype(F32)
        out[z + half] = (own[z + half].astype(F32) + high).astype(BF16)


def step_y(value, step):
    pairs = [(i, ((i // NZ + step) % NY) * NZ + i % NZ) for i in range(COL)]
    return lax.ppermute(value, "col", pairs)


def thirds(value):
    high = value.astype(BF16)
    rest = value - high.astype(F32)
    middle = rest.astype(BF16)
    return high, middle, (rest - middle.astype(F32)).astype(BF16)


def dense_kernel(parts, dest_scale, weight, bias, targets, upstream, hidden, packed):
    summed = parts[0].astype(F32)
    for z in range(1, NZ):
        summed = summed + parts[z].astype(F32)
    scale = column(dest_scale[...])
    aggregated = (summed * scale).astype(BF16)
    w = weight[...]
    preact = jnp.dot(aggregated, w, preferred_element_type=F32) + bias[...]
    hidden[...] = (preact * sigmoid(preact)).astype(BF16)
    wanted = targets[...]
    row_ids = lax.broadcasted_iota(jnp.int32, (BLK, TGT), 0)
    chosen = (row_ids == wanted).astype(BF16)
    agg_t = lax.dot_general(
        chosen, aggregated, (((0,), (0,)), ((), ())), preferred_element_type=F32
    ).astype(BF16)
    pre_t = jnp.dot(agg_t, w, preferred_element_type=F32) + bias[...]
    s = sigmoid(pre_t)
    slope = (upstream[...].astype(F32) * (s * (1.0 + pre_t * (1.0 - s)))).astype(BF16)
    weight_part = lax.dot_general(
        agg_t, slope, (((0,), (0,)), ((), ())), preferred_element_type=F32
    )
    bias_part = jnp.sum(slope.astype(F32), axis=0, keepdims=True)
    term = lax.dot_general(
        slope, w, (((1,), (1,)), ((), ())), preferred_element_type=F32
    )
    same = lax.dot_general(
        chosen, chosen, (((0,), (0,)), ((), ())), preferred_element_type=F32
    )
    collected = sum(
        jnp.dot(same.astype(BF16), third, preferred_element_type=F32) for third in thirds(term)
    )
    scale_t = sum(
        lax.dot_general(chosen, third, (((0,), (0,)), ((), ())), preferred_element_type=F32)
        for third in thirds(scale)
    )
    k_row = lax.broadcasted_iota(jnp.int32, (TGT, TGT), 0)
    k_col = lax.broadcasted_iota(jnp.int32, (TGT, TGT), 1)
    earlier = jnp.sum(jnp.where(k_col < k_row, same, 0.0), axis=1, keepdims=True)
    returned = jnp.where(earlier > 0.0, 0.0, collected * scale_t).astype(BF16)
    names = jnp.concatenate([wanted.astype(F32)] * (BLK // TGT), axis=1)
    lanes = lax.broadcasted_iota(jnp.int32, (1, BLK), 1)
    names = jnp.where(lanes // TGT == (lax.axis_index("col") & 3), names, -1.0)
    high = bias_part.astype(BF16).astype(F32)
    low = bias_part - high
    sundry = jnp.concatenate(
        [names, high[:, :BLK], high[:, BLK:], low[:, :BLK], low[:, BLK:], jnp.zeros((3, BLK), F32)],
        axis=0,
    )
    for c in range(COL):
        at, side = 8 * (c // 2), BLK * (c % 2)
        chunk = weight_part[at : at + 8, side : side + BLK]
        packed[c, 0:TGT, :] = returned
        packed[c, TGT:, :] = jnp.concatenate([chunk, sundry], axis=0).astype(BF16)


def gradient_kernel(packed, chunks, bias):
    total = packed[0, TGT:, :].astype(F32)
    for c in range(1, COL):
        total = total + packed[c, TGT:, :].astype(F32)
    for c in range(COL):
        chunks[c] = total[0:8, :]
    bias[...] = jnp.concatenate([total[9:10] + total[11:12], total[10:11] + total[12:13]], axis=1)


def unpack(packed, returned):
    row_ids = lax.broadcasted_iota(jnp.int32, (BLK, BLK), 0).astype(F32)
    quarters = BLK // TGT
    for g in range(COL // quarters):
        held = slice(g * quarters, (g + 1) * quarters)
        rows = jnp.transpose(packed[held, 0:TGT, :].reshape(BLK, F))
        for first in range(g * quarters, (g + 1) * quarters, 2):
            chosen = [
                (row_ids == packed[c, TGT:, :].astype(F32)[8:9, :]).astype(BF16)
                for c in (first, first + 1)
            ]
            placed = lax.dot_general(
                rows,
                jnp.concatenate(chosen, axis=0),
                (((1,), (1,)), ((), ())),
                preferred_element_type=F32,
            ).astype(BF16)
            returned[first] = placed[:, :BLK]
            returned[first + 1] = placed[:, BLK:]


def bias_rows(bias):
    high = bias.astype(BF16).astype(F32)
    low = bias - high
    return jnp.concatenate(
        [high[:, :BLK], high[:, BLK:], low[:, :BLK], low[:, BLK:], jnp.zeros((12, BLK), F32)],
        axis=0,
    ).astype(BF16)


def bias_of(rows):
    rows = rows.astype(F32)
    return jnp.concatenate([rows[0:1] + rows[2:3], rows[1:2] + rows[3:4]], axis=1)


def backward_kernel(ids, mask, packed, bias, own, other, returned, totals, *work):
    numbers, staged = work[:2]
    wait_numbers, wait_tiles = stream(ids, mask, *work)
    my_core = lax.axis_index("dom") & 1
    for ref in (own, other):
        ref[NX * 256 :, :] = bias_rows(bias[...])
    unpack(packed, returned)
    totals[...] = jnp.zeros_like(totals)
    wait_numbers()

    def step(i, carry):
        wait_tiles(i)
        for u in range(STEP):
            t = i * STEP + u
            r, c = numbers[t] >> 4, numbers[t] & 15
            tile = staged[t].astype(F32).astype(BF16)
            totals[c] = totals[c] + jnp.dot(returned[r], tile, preferred_element_type=F32)
        return carry

    lax.fori_loop(0, mask.shape[0] // STEP, step, 0)
    for x in range(NX):
        for half in range(2):
            rows_at = pl.ds(x * 256 + half * BLK, BLK)
            for ref, core in ((own, my_core), (other, 1 - my_core)):
                block = (x * NCORE + core) * 2 + half
                ref[rows_at, :] = jnp.transpose(totals[block]).astype(BF16)


def core_sum_kernel(own, got, grads, grads_got, out):
    at = NX * 256
    bias = bias_rows(bias_of(own[at:, :]) + bias_of(got[at:, :]))
    weight_sum = [(grads[c] + grads_got[c]).astype(BF16) for c in range(COL)]
    for x in range(NX):
        rows_at = slice(x * 256, (x + 1) * 256)
        total = own[rows_at, :].astype(F32) + got[rows_at, :].astype(F32)
        out[x, 0:256, :] = total.astype(BF16)
        for c in range(0, COL, 2):
            out[x, 256 + 8 * c : 272 + 8 * c, :] = jnp.concatenate(weight_sum[c : c + 2], axis=0)
        out[x, 256 + HID :, :] = bias


def finish_kernel(parts, source_scale, grad, weight_grad, bias_grad):
    def total(at):
        return (parts[0, at, :].astype(F32) + parts[1, at, :].astype(F32)) + (
            parts[2, at, :].astype(F32) + parts[3, at, :].astype(F32)
        )

    for half in range(2):
        at = slice(half * BLK, (half + 1) * BLK)
        grad[at, :] = total(at) * column(source_scale[:, at])
    for c in range(0, COL, 2):
        both = total(slice(256 + 8 * c, 272 + 8 * c))
        rows_at = slice(4 * c, 4 * c + 8)
        weight_grad[rows_at, :BLK] = both[0:8]
        weight_grad[rows_at, BLK:] = both[8:16]
    bias = [bias_of(parts[x, 256 + HID :, :]) for x in range(NX)]
    bias_grad[...] = (bias[0] + bias[1]) + (bias[2] + bias[3])


def body(
    source_feats,
    source_scale,
    dest_scale,
    weight,
    layer_bias,
    tile_rows,
    tile_cols,
    tile_mask,
    targets,
    upstream,
):
    scaled = (source_feats.astype(F32) * source_scale[:, None]).astype(BF16)
    along_x = [scaled] + [exchange_dom(scaled, NCORE * k) for k in range(1, NX)]
    pieces = [piece for held in along_x for piece in (held, exchange_dom(held, 1))]
    products = 2 * tile_mask.shape[0] * BLK**3
    ids = tile_rows * 16 + tile_cols
    own, far_up, far_down, up_low, up_high, down_low, down_high = forward(ids, tile_mask, pieces)
    far_up, far_down = step_y(far_up, 1), step_y(far_down, -1)
    high_below, low_above = step_y(up_high, 1), step_y(down_low, -1)
    up, down = call(relay_kernel, [sds((NZ // 2, BLK, F), BF16)] * 2, [VMEM] * 4)(
        up_low, far_up, down_high, far_down
    )
    low_below, high_above = step_y(up, 1), step_y(down, -1)
    (line,) = call(y_sum_kernel, [sds((NZ, BLK, F), BF16)], [VMEM] * 5)(
        own, low_above, low_below, high_below, high_above
    )
    parts = swap(line, "col", Z_GROUPS)
    hidden, packed = call(
        dense_kernel,
        [sds((BLK, HID), BF16), sds((COL, PACK, F), BF16)],
        [VMEM] * 6,
    )(
        parts,
        dest_scale.reshape(1, BLK),
        weight,
        layer_bias.reshape(1, HID),
        targets.reshape(1, TGT),
        upstream,
    )
    gathered = swap(packed, "col")
    chunks, bias_sum = call(
        gradient_kernel, [sds((COL, 8, BLK), F32), sds((1, HID), F32)], [VMEM]
    )(gathered)
    grads = swap(chunks, "col")
    own, other = call(
        backward_kernel,
        [sds((NX * 256 + 16, F), BF16)] * 2,
        [HBM, HBM, VMEM, VMEM],
        [pltpu.VMEM((COL, F, BLK), BF16), pltpu.VMEM((DOM * 2, F, BLK), F32)]
        + stream_scratch(tile_mask),
        flops=products,
        limit=52,
    )(ids, tile_mask, gathered, bias_sum)
    got = exchange_dom(other, 1)
    grads_got = exchange_dom(grads, 1)
    (by_x,) = call(core_sum_kernel, [sds((NX, 256 + GRADS, F), BF16)], [VMEM] * 4)(
        own, got, grads, grads_got
    )
    input_grad, weight_grad, bias_grad = call(
        finish_kernel,
        [sds((256, F), F32), sds((F, HID), F32), sds((1, HID), F32)],
        [VMEM] * 2,
    )(swap(by_x, "dom", X_GROUPS), source_scale.reshape(1, 256))
    return hidden, weight_grad, bias_grad.reshape(HID), input_grad


def solution(mesh):
    placed = (
        P(("col", "dom"), None),
        P(("col", "dom")),
        P(("col", "dom")),
        P(),
        P(),
        P(("col", "dom")),
        P(("col", "dom")),
        P(("col", "dom"), None, None),
        P(("col", "dom")),
        P(("col", "dom"), None),
    )
    return jax.shard_map(
        body,
        mesh=mesh,
        in_specs=placed,
        out_specs=(P(("col", "dom"), None), P(), P(), P(("col", "dom"), None)),
        check_vma=False,
    )
```
